512 devices in a mesh: dp: 64 (over x, z, core), mp: 8 (over y).
Axes of the slice: x: 4, y: 8, z: 8, core: 2. Of those that a mesh axis runs over, the one named last changes fastest.
Arguments:
- child_queries: bfloat16 [64, 4, 128, 64, 128], P('dp', None, None, 'mp'), may hold values from -72 to 72
- child_keys: bfloat16 [64, 4, 128, 8, 128], P('dp', None, None, 'mp'), may hold values from -5 to 5
- child_values: bfloat16 [64, 4, 128, 8, 128], P('dp', None, None, 'mp'), may hold values from -36 to 36
- prefix_keys: bfloat16 [64, 2048, 8, 128], P('dp', None, 'mp'), may hold values from -6.25 to 6.25
- prefix_values: bfloat16 [64, 2048, 8, 128], P('dp', None, 'mp'), may hold values from -36 to 36
- child_count: int32 [64], P('dp'), may hold values from 1 to 4, as said below
- child_parent: int32 [64, 4], P('dp'), may hold values from 0 to 63, as said below
- reward_weight: bfloat16 [64, 128, 2], P('mp'), may hold values from -0.14941406 to 0.14941406
Outputs:
- attended: bfloat16 [64, 4, 128, 64, 128], P('dp', None, None, 'mp')
- reward_logits: float32 [64, 4, 128, 2], P('dp')
The draws below stay inside these ranges and needn't reach their ends.
Inputs may be any that keep to these rules, and one draw needn't show every extreme that they name: `child_count`: 4 is reached on some index of dp in every draw. `child_parent`: the parent of a child in row p is one of p, p - 1, ..., p - 3, taken modulo 64.
All inputs are finite; a program needn't handle non-finite values.
Results may differ from the reference program's by a relative error of at most 0.014.
Values may be sent and summed in bfloat16 or wider, within the bound.
A program may use at most 128 MiB of HBM per device.

```python
import jax
import jax.numpy as jnp
from jax import lax

HEADS = 64
KVH = 8
HD = 128
PREFIX = 2048
STEP = 128
CAP = 4
WINDOW = 4
PARENTS = 64


def unit_keys(key):
    values = jax.random.normal(key, (PARENTS, CAP, STEP, KVH, HD), jnp.float32)
    return jnp.clip(values, -4.0, 4.0)


def unit_prefix(key):
    own_key = jax.random.fold_in(key, 31)
    values = jax.random.normal(own_key, (PARENTS, PREFIX, KVH, HD), jnp.float32)
    return jnp.clip(values, -5.0, 5.0)


def parent_table(key):
    own_key = jax.random.fold_in(key, 22)
    distance = jax.random.randint(own_key, (PARENTS, CAP), 0, WINDOW)
    owners = jnp.arange(PARENTS, dtype=jnp.int32)[:, None]
    return jnp.mod(owners - distance, PARENTS).astype(jnp.int32)


def draw_child_keys(key, part):
    shared = unit_keys(key)
    return (1.25 * shared).astype(jnp.bfloat16)


def draw_prefix_keys(key, part):
    shared = unit_prefix(key)
    return (1.25 * shared).astype(jnp.bfloat16)


def draw_child_queries(key, part):
    key = jax.random.fold_in(key, 11)
    first = jax.random.fold_in(key, 0)
    queries = 1.25 * jax.random.normal(first, (PARENTS, CAP, STEP, HEADS, HD), jnp.float32)
    queries = jnp.clip(queries, -6.0, 6.0)
    return queries.astype(jnp.bfloat16)


def draw_child_count(key, part):
    key = jax.random.fold_in(key, 21)
    first, second, third = jax.random.split(key, 3)
    crowded = jax.random.randint(first, (PARENTS,), 0, 4) == 0
    sparse = jax.random.randint(second, (PARENTS,), 1, 3)
    counts = jnp.where(crowded, CAP, sparse).astype(jnp.int32)
    chosen = jax.random.randint(third, (), 0, PARENTS)
    return counts.at[chosen].set(CAP).astype(jnp.int32)


def draw_child_parent(key, part):
    table = parent_table(key)
    return table


def levels(stream_key, shape, shards, smallest, top_value):
    loudness = 1.0
    for axis_at, blocks in shards:
        heights = jax.random.uniform(jax.random.fold_in(jax.random.fold_in(stream_key, 6), axis_at), (blocks,), jnp.float32, smallest / len(shards), top_value / len(shards))
        loudness = loudness * jnp.repeat(jnp.exp(heights), shape[axis_at] // blocks).reshape((-1,) + (1,) * (len(shape) - 1 - axis_at))
    return loudness


def normal_values(stream_key, shape, width, most, cuts=(), kind=jnp.bfloat16):
    drawn = width * jax.random.normal(stream_key, shape, jnp.float32)
    if cuts:
        drawn = drawn * levels(stream_key, shape, cuts, -0.22, 0.18)
    return jnp.clip(drawn, -most, most).astype(kind)


def setup_inputs(seed: int = 0) -> dict:
    keys = jax.random.split(jax.random.key(seed), 9)
    child_queries = draw_child_queries(jax.random.fold_in(keys[8], 71), 0)
    child_keys = draw_child_keys(jax.random.fold_in(keys[8], 71), 0)
    child_values = normal_values(keys[2], (PARENTS, CAP, STEP, KVH, HD), 6.0, 36.0, ((0, 64), (3, 8)))
    prefix_keys = draw_prefix_keys(jax.random.fold_in(keys[8], 71), 0)
    prefix_values = normal_values(keys[4], (PARENTS, PREFIX, KVH, HD), 6.0, 36.0, ((0, 64), (2, 8)))
    child_count = draw_child_count(jax.random.fold_in(keys[8], 71), 0)
    child_parent = draw_child_parent(jax.random.fold_in(keys[8], 71), 0)
    reward_weight = normal_values(keys[7], (HEADS, HD, 2), 0.025, 0.14941406, ((0, 8),))
    return dict(child_queries=child_queries, child_keys=child_keys, child_values=child_values, prefix_keys=prefix_keys, prefix_values=prefix_values, child_count=child_count, child_parent=child_parent, reward_weight=reward_weight)


neg_large = -1.0e30


def reference(child_queries, child_keys, child_values, prefix_keys, prefix_values, child_count, child_parent, reward_weight):
    groups = HEADS // KVH
    members = PARENTS * CAP
    flat_queries = child_queries.reshape(members, STEP, HEADS, HD)
    flat_keys = child_keys.reshape(members, STEP, KVH, HD)
    flat_values = child_values.reshape(members, STEP, KVH, HD)
    flat_parent = child_parent.reshape(members)
    slot_pos = jnp.arange(CAP, dtype=jnp.int32)
    flat_active = (slot_pos[None, :] < child_count[:, None]).reshape(members)
    row_pos = jnp.arange(STEP, dtype=jnp.int32)
    visible = jnp.concatenate([jnp.ones((STEP, PREFIX), dtype=bool), row_pos[None, :] <= row_pos[:, None]], axis=1)

    def one_child(member):
        parent = flat_parent[member]
        key_rows = jnp.concatenate([prefix_keys[parent], flat_keys[member]], axis=0).astype(jnp.float32)
        value_rows = jnp.concatenate([prefix_values[parent], flat_values[member]], axis=0).astype(jnp.float32)
        grouped = flat_queries[member].astype(jnp.float32).reshape(STEP, KVH, groups, HD)
        scores = jnp.einsum("tkgd,skd->kgts", grouped, key_rows) * (HD ** -0.5)
        scores = jnp.where(visible, scores, neg_large)
        row_peak = jnp.max(scores, axis=-1, keepdims=True)
        weights = jnp.exp(scores - row_peak)
        row_total = jnp.sum(weights, axis=-1)
        rounded = lax.optimization_barrier(weights.astype(jnp.bfloat16)).astype(jnp.float32)
        weighted = jnp.einsum("kgts,skd->tkgd", rounded, value_rows)
        normed = weighted / jnp.transpose(row_total, (2, 0, 1))[..., None]
        return normed.reshape(STEP, HEADS, HD).astype(jnp.bfloat16)

    def empty_child(member):
        return jnp.zeros((STEP, HEADS, HD), jnp.bfloat16)

    def guarded(member):
        return lax.cond(flat_active[member], one_child, empty_child, member)

    attended = lax.map(guarded, jnp.arange(members, dtype=jnp.int32))
    logits = jnp.einsum("nthd,hdz->ntz", attended.astype(jnp.float32), reward_weight.astype(jnp.float32))
    return attended.reshape(PARENTS, CAP, STEP, HEADS, HD), logits.reshape(PARENTS, CAP, STEP, 2)
```

```python
import functools

import jax
import jax.numpy as jnp
from jax import lax
from jax.experimental import pallas as pl
from jax.experimental.pallas import tpu as pltpu
from jax.sharding import PartitionSpec as P

MESH = pl.DeviceIdType.MESH
CHUNKS = 8
AHEAD = 2
COLS = 256
LOG2E = 1.4426950408889634
NEG = -1.0e30


def kernel(
    n_dp,
    n_mp,
    q_hbm,
    ck_hbm,
    cv_hbm,
    pk_hbm,
    pv_hbm,
    w_ref,
    count_ref,
    parent_ref,
    att_ref,
    logit_ref,
    *scratch,
):
    bufs = scratch[:CHUNKS]
    (q_ref, ck_ref, cv_ref, acc_ref, m_ref, l_ref, part_ref, gather_ref) = scratch[CHUNKS : CHUNKS + 8]
    (in_sem, own_sem, recv_sem, z_sem, d2d_sem, fwd_sem, y_send, y_recv) = scratch[CHUNKS + 8 :]
    slots, rows, size = q_ref.shape
    chunk = bufs[0].shape[2]
    heads = w_ref.shape[0] // 2
    scale = LOG2E * size**-0.5

    dp = lax.axis_index("dp")
    mp = lax.axis_index("mp")
    core = lax.rem(dp, 2)
    mate = dp + 1 - 2 * core
    ahead = lax.rem(dp + 2, n_dp)
    behind = lax.rem(dp + n_dp - 2, n_dp)
    cross = lax.rem(dp + n_dp + 2 * core - 1, n_dp)

    loads = [
        pltpu.make_async_copy(q_hbm, q_ref, in_sem.at[0]),
        pltpu.make_async_copy(ck_hbm, ck_ref, in_sem.at[1]),
        pltpu.make_async_copy(cv_hbm, cv_ref, in_sem.at[2]),
    ]
    for copy in loads:
        copy.start()

    def part(j):
        return pl.ds(j * chunk, chunk)

    sources = (pk_hbm, pv_hbm)

    def own(j, kind):
        return pltpu.make_async_copy(sources[kind].at[part(j)], bufs[j].at[0, kind], own_sem.at[j, kind])

    barrier = pltpu.get_barrier_semaphore()
    for other in (mate, ahead, behind, cross):
        pl.semaphore_signal(barrier, inc=1, device_id=(other, mp), device_id_type=MESH)
    for step in range(1, n_mp):
        pl.semaphore_signal(barrier, inc=1, device_id=(dp, lax.rem(mp + step, n_mp)), device_id_type=MESH)
    for j in range(CHUNKS):
        for kind in (0, 1):
            own(j, kind).start()
    pl.semaphore_wait(barrier, 4 + n_mp - 1)

    def remote(src, j, slot, kind, sem, target):
        return pltpu.make_async_remote_copy(
            src_ref=src,
            dst_ref=bufs[j].at[slot, kind],
            send_sem=sem,
            recv_sem=recv_sem.at[slot - 1, j, kind],
            device_id=(target, mp),
            device_id_type=MESH,
        )

    def z_send(j, kind):
        return remote(sources[kind].at[part(j)], j, 2, kind, z_sem.at[j, kind], ahead)

    def own_to_mate(j, kind):
        return remote(sources[kind].at[part(j)], j, 1, kind, d2d_sem.at[j, kind], mate)

    def two_to_mate(j, kind, slot):
        return remote(bufs[j].at[2, kind], j, slot, kind, fwd_sem.at[j, kind], mate)

    def two_to_next(j, kind):
        return remote(bufs[j].at[2, kind], j, 3, kind, d2d_sem.at[j, kind], cross)

    def wait_slot(j, slot):
        for kind in (0, 1):
            remote(bufs[j].at[slot, kind], j, slot, kind, z_sem.at[j, kind], mate).wait_recv()

    def start_z(j):
        for kind in (0, 1):
            z_send(j, kind).start()

        @pl.when(core == 0)
        def _():
            for kind in (0, 1):
                own_to_mate(j, kind).start()

    def forward(j):
        @pl.when(core == 0)
        def _():
            for kind in (0, 1):
                two_to_mate(j, kind, 3).start()

        @pl.when(core == 1)
        def _():
            for kind in (0, 1):
                two_to_next(j, kind).start()
            for kind in (0, 1):
                two_to_mate(j, kind, 1).start()

    for j in range(AHEAD):
        start_z(j)

    for copy in loads:
        copy.wait()

    def first(c, _):
        keys = ck_ref[c]
        values = cv_ref[c].T
        for start in range(0, rows, COLS):
            cols = pl.ds(start, COLS)
            s = lax.dot_general(keys, q_ref[c, cols], (((1,), (1,)), ((), ())), preferred_element_type=jnp.float32)
            key_at = lax.broadcasted_iota(jnp.int32, s.shape, 0)
            row_at = (lax.broadcasted_iota(jnp.int32, s.shape, 1) + start) // heads
            s = jnp.where(key_at <= row_at, s, NEG)
            peak = jnp.max(s, axis=0, keepdims=True)
            p = jnp.exp2((s - peak) * scale)
            m_ref[c, :, cols] = peak
            l_ref[c, :, cols] = jnp.sum(p, axis=0, keepdims=True)
            acc_ref[c, :, cols] = jnp.dot(values, p.astype(jnp.bfloat16), preferred_element_type=jnp.float32)
        return 0

    lax.fori_loop(0, slots, first, 0)

    def compute(j):
        for kind in (0, 1):
            own(j, kind).wait()
        wait_slot(j, 1)
        wait_slot(j, 3)

        def one(c, _):
            distance = jnp.bitwise_and(dp - parent_ref[0, c], 3)
            keys = bufs[j][distance, 0]
            values = bufs[j][distance, 1].T
            for start in range(0, rows, COLS):
                cols = pl.ds(start, COLS)
                s = lax.dot_general(keys, q_ref[c, cols], (((1,), (1,)), ((), ())), preferred_element_type=jnp.float32)
                old = m_ref[c, :, cols]
                peak = jnp.maximum(old, jnp.max(s, axis=0, keepdims=True))
                p = jnp.exp2((s - peak) * scale)
                alpha = jnp.exp2((old - peak) * scale)
                m_ref[c, :, cols] = peak
                l_ref[c, :, cols] = l_ref[c, :, cols] * alpha + jnp.sum(p, axis=0, keepdims=True)
                acc_ref[c, :, cols] = acc_ref[c, :, cols] * alpha + jnp.dot(
                    values, p.astype(jnp.bfloat16), preferred_element_type=jnp.float32
                )
            return 0

        lax.fori_loop(0, slots, one, 0)

    for j in range(CHUNKS):
        wait_slot(j, 2)
        forward(j)
        if j + AHEAD < CHUNKS:
            start_z(j + AHEAD)
        if j >= 1:
            compute(j - 1)
    compute(CHUNKS - 1)

    weight = w_ref[...]
    head_at = lax.broadcasted_iota(jnp.int32, (rows, 2 * heads), 0) % heads
    weight_at = lax.broadcasted_iota(jnp.int32, (rows, 2 * heads), 1) // 2
    same = head_at == weight_at
    pick = (
        lax.broadcasted_iota(jnp.int32, (2, 2 * heads), 0) == lax.broadcasted_iota(jnp.int32, (2, 2 * heads), 1) % 2
    ).astype(jnp.float32)

    def last(c, _):
        live = c < count_ref[0]
        done = acc_ref[c] * (1.0 / l_ref[c])
        done = jnp.where(live, done, 0.0).astype(jnp.bfloat16).T
        att_ref[c] = done
        z = lax.dot_general(done, weight, (((1,), (1,)), ((), ())), preferred_element_type=jnp.float32)
        z = jnp.where(same, z, 0.0).reshape(rows // heads, heads, 2 * heads)
        z = jnp.sum(z, axis=1)
        part_ref[c] = lax.dot_general(
            pick, z, (((1,), (1,)), ((), ())), preferred_element_type=jnp.float32, precision=lax.Precision.HIGHEST
        )
        return 0

    lax.fori_loop(0, slots, last, 0)

    def to_peer(step):
        return pltpu.make_async_remote_copy(
            src_ref=part_ref,
            dst_ref=gather_ref.at[step - 1],
            send_sem=y_send.at[step - 1],
            recv_sem=y_recv.at[step - 1],
            device_id=(dp, lax.rem(mp + step, n_mp)),
            device_id_type=MESH,
        )

    for step in range(1, n_mp):
        to_peer(step).start()
    total = part_ref[...]
    for step in range(1, n_mp):
        to_peer(step).wait_recv()
        total = total + gather_ref[step - 1]
    logit_ref[...] = total

    for step in range(1, n_mp):
        to_peer(step).wait_send()
    for j in range(CHUNKS):
        for kind in (0, 1):
            z_send(j, kind).wait_send()
            own_to_mate(j, kind).wait_send()
            two_to_mate(j, kind, 3).wait_send()


def solution(mesh):
    n_dp, n_mp = mesh.shape["dp"], mesh.shape["mp"]

    def step(queries, keys, values, prefix_keys, prefix_values, count, parent, weight):
        _, slots, steps, heads, size = queries.shape
        prefix = prefix_keys.shape[1]
        rows = steps * heads
        chunk = prefix // CHUNKS
        hbm = pl.BlockSpec(memory_space=pl.ANY)
        vmem = pl.BlockSpec(memory_space=pltpu.VMEM)
        smem = pl.BlockSpec(memory_space=pltpu.SMEM)
        bf16, f32 = jnp.bfloat16, jnp.float32
        attended, logits = pl.pallas_call(
            functools.partial(kernel, n_dp, n_mp),
            out_shape=(
                jax.ShapeDtypeStruct((slots, rows, size), bf16),
                jax.ShapeDtypeStruct((slots, 2, steps), f32),
            ),
            in_specs=[hbm, hbm, hbm, hbm, hbm, vmem, smem, smem],
            out_specs=(vmem, vmem),
            scratch_shapes=[pltpu.VMEM((4, 2, chunk, size), bf16)] * CHUNKS
            + [
                pltpu.VMEM((slots, rows, size), bf16),
                pltpu.VMEM((slots, steps, size), bf16),
                pltpu.VMEM((slots, steps, size), bf16),
                pltpu.VMEM((slots, size, rows), f32),
                pltpu.VMEM((slots, 1, rows), f32),
                pltpu.VMEM((slots, 1, rows), f32),
                pltpu.VMEM((slots, 2, steps), f32),
                pltpu.VMEM((n_mp - 1, slots, 2, steps), f32),
                pltpu.SemaphoreType.DMA((3,)),
                pltpu.SemaphoreType.DMA((CHUNKS, 2)),
                pltpu.SemaphoreType.DMA((3, CHUNKS, 2)),
                pltpu.SemaphoreType.DMA((CHUNKS, 2)),
                pltpu.SemaphoreType.DMA((CHUNKS, 2)),
                pltpu.SemaphoreType.DMA((CHUNKS, 2)),
                pltpu.SemaphoreType.DMA((n_mp - 1,)),
                pltpu.SemaphoreType.DMA((n_mp - 1,)),
            ],
            compiler_params=pltpu.CompilerParams(
                collective_id=0, has_side_effects=True, vmem_limit_bytes=48 * 1024 * 1024
            ),
            name="prefix_attention",
        )(
            queries.reshape(slots, rows, size),
            keys.reshape(slots, steps, size),
            values.reshape(slots, steps, size),
            prefix_keys.reshape(prefix, size),
            prefix_values.reshape(prefix, size),
            jnp.transpose(weight, (0, 2, 1)).reshape(2 * heads, size),
            count,
            parent,
        )
        attended = attended.reshape(1, slots, steps, heads, size)
        return attended, jnp.transpose(logits, (0, 2, 1))[None]

    return jax.shard_map(
        step,
        mesh=mesh,
        in_specs=(
            P("dp", None, None, "mp", None),
            P("dp", None, None, "mp", None),
            P("dp", None, None, "mp", None),
            P("dp", None, "mp", None),
            P("dp", None, "mp", None),
            P("dp"),
            P("dp", None),
            P("mp", None, None),
        ),
        out_specs=(P("dp", None, None, "mp", None), P("dp", None, None, None)),
        check_vma=False,
    )
```

```python
import functools

import jax
import jax.numpy as jnp
from jax import lax
from jax.experimental import pallas as pl
from jax.experimental.pallas import tpu as pltpu
from jax.sharding import PartitionSpec as P

MESH = pl.DeviceIdType.MESH
SIZES = (8, 8, 8, 8, 8, 8, 8, 8)
DETOUR = ()
RELAY = ((0, 1, 2), (3, 4, 5), (6, 7), (), (), (), (), ())
AHEAD = 4
COLS = 256
EXTRA = 16
RING = 8
LOG2E = 1.4426950408889634
NEG = -1.0e30
VMEM_LIMIT = 60 * 1024 * 1024


def kernel(n_dp, n_mp, q_hbm, ck_hbm, cv_hbm, pk_hbm, pv_hbm, w_hbm, count_hbm, parent_hbm, att_ref, logit_ref, *scratch):
    scratch = list(scratch)

    def take(n):
        taken, scratch[:n] = scratch[:n], []
        return taken

    chunks = len(SIZES)
    bufs, relays = take(chunks), take(chunks)
    q_ref, ck_ref, cv_ref, w_ref, count_ref, parent_ref = take(6)
    acc_ref, m_ref, qq_ref, part_ref, gather_ref, z_ref, vt_ref, member_ref, done_ref = take(9)
    s_ref, top_ref, p_ref, alpha_ref = take(4)
    in_sem, own_sem, recv_sem, z_sem, d2d_sem, fwd_sem, out_sem, relay_sem, pass_sem, y_send, y_recv = scratch

    slots, rows, size = q_ref.shape
    prefix = pk_hbm.shape[0]
    heads = w_ref.shape[0] // 2
    blocks = rows // COLS
    scale = LOG2E * size**-0.5
    sizes = [prefix * n // sum(SIZES) for n in SIZES]
    most = max(sizes)
    starts = [sum(sizes[:j]) for j in range(chunks)]

    dp = lax.axis_index("dp")
    mp = lax.axis_index("mp")
    core = lax.rem(dp, 2)
    z = lax.rem(dp // 2, RING)
    plane = dp // (2 * RING)
    planes = n_dp // (2 * RING)

    def at(x, chip, which):
        return (lax.rem(x + planes, planes) * RING + chip) * 2 + which

    mate = dp + 1 - 2 * core
    ahead = lax.rem(dp + 2, n_dp)
    behind = lax.rem(dp + n_dp - 2, n_dp)
    cross = lax.rem(dp + n_dp + 2 * core - 1, n_dp)
    via = at(plane + (z + 2) // RING, lax.rem(z + RING - 3, RING), 1)
    served = lax.rem(z + 3, RING)
    served_from = at(plane - (served + 2) // RING, served, 1)
    drop = at(plane, lax.rem(served + 2, RING), 0)
    brought = at(plane, lax.rem(z + 3, RING), 1)

    sources = (pk_hbm, pv_hbm)

    def part(j):
        return pl.ds(starts[j], sizes[j])

    def own(j, kind):
        return pltpu.make_async_copy(sources[kind].at[part(j)], bufs[j].at[0, kind], own_sem.at[j])

    def own_whole(j):
        return pltpu.make_async_copy(bufs[j].at[1], bufs[j].at[0], own_sem.at[j])

    loads = [
        pltpu.make_async_copy(src, dst, in_sem.at[k])
        for k, (src, dst) in enumerate(
            (
                (parent_hbm, parent_ref),
                (count_hbm, count_ref),
                (q_hbm, q_ref),
                (ck_hbm, ck_ref),
                (cv_hbm, cv_ref),
                (w_hbm, w_ref),
            )
        )
    ]

    barrier = pltpu.get_barrier_semaphore()

    def greet(*others):
        for other in others:
            pl.semaphore_signal(barrier, inc=1, device_id=(other, mp), device_id_type=MESH)

    greet(mate, ahead, behind, cross)
    for step in range(1, n_mp):
        pl.semaphore_signal(barrier, inc=1, device_id=(dp, lax.rem(mp + step, n_mp)), device_id_type=MESH)

    @pl.when(core == 0)
    def _():
        greet(brought)

    @pl.when(core == 1)
    def _():
        greet(via, served_from, drop)

    for copy in loads:
        copy.start()
    for j in range(chunks):
        for kind in (0, 1):
            own(j, kind).start()
    pl.semaphore_wait(barrier, 4 + n_mp - 1 + 1 + 2 * core)

    def remote(src, dst, send, recv, target):
        return pltpu.make_async_remote_copy(
            src_ref=src, dst_ref=dst, send_sem=send, recv_sem=recv, device_id=(target, mp), device_id_type=MESH
        )

    def to_ahead(j, kind):
        return remote(sources[kind].at[part(j)], bufs[j].at[2, kind], z_sem.at[j], recv_sem.at[1, j], ahead)

    def own_to_mate(j, kind):
        return remote(sources[kind].at[part(j)], bufs[j].at[1, kind], d2d_sem.at[j], recv_sem.at[0, j], mate)

    def own_to_via(j, kind):
        return remote(sources[kind].at[part(j)], relays[j].at[kind], out_sem.at[j], relay_sem.at[j], via)

    def two_to_mate(j, slot):
        return remote(bufs[j].at[2], bufs[j].at[slot], fwd_sem.at[j], recv_sem.at[slot - 1, j], mate)

    def two_to_next(j):
        return remote(bufs[j].at[2], bufs[j].at[3], d2d_sem.at[j], recv_sem.at[2, j], cross)

    def relay_on(j):
        return remote(relays[j], bufs[j].at[3], pass_sem.at[j], recv_sem.at[2, j], drop)

    def whole(j, send, recv):
        return remote(bufs[j].at[2], bufs[j].at[1], send, recv, mate)

    def wait_slot(j, slot):
        whole(j, z_sem.at[j], recv_sem.at[slot - 1, j]).wait_recv()

    def wait_sent(j, sem):
        whole(j, sem.at[j], recv_sem.at[0, j]).wait_send()

    def on_ring(j, owner, do):
        if j in DETOUR:
            do()
        else:
            pl.when(lax.rem(owner + 2, RING) == 0)(do)

    def off_ring(j, owner, do):
        if j not in DETOUR:
            pl.when(lax.rem(owner + 2, RING) != 0)(do)

    def start_direct(j):
        for kind in (0, 1):
            to_ahead(j, kind).start()

        @pl.when(core == 0)
        def _():
            for kind in (0, 1):
                own_to_mate(j, kind).start()

    def start_detour(j):
        def do():
            for kind in (0, 1):
                own_to_via(j, kind).start()

        on_ring(j, z, do)

    def pass_on(j):
        def do():
            remote(relays[j], relays[j], out_sem.at[j], relay_sem.at[j], via).wait_recv()
            relay_on(j).start()

        on_ring(j, served, do)

    def forward(j):
        @pl.when(core == 0)
        def _():
            two_to_mate(j, 3).start()

        @pl.when(core == 1)
        def _():
            two_to_mate(j, 1).start()
            off_ring(j, lax.rem(z + RING - 1, RING), lambda: two_to_next(j).start())

    def settle(j):
        wait_sent(j, z_sem)
        wait_sent(j, fwd_sem)

        @pl.when(core == 0)
        def _():
            wait_sent(j, d2d_sem)

        @pl.when(core == 1)
        def _():
            off_ring(j, lax.rem(z + RING - 1, RING), lambda: wait_sent(j, d2d_sem))
            on_ring(j, z, lambda: wait_sent(j, out_sem))
            on_ring(j, served, lambda: wait_sent(j, pass_sem))

    start_direct(0)

    @pl.when(core == 1)
    def _():
        for j in range(chunks):
            start_detour(j)

    for j in range(1, AHEAD):
        start_direct(j)
    eager = lax.rem(z + 1, RING) <= 1

    @pl.when(eager)
    def _():
        for j in range(AHEAD, chunks):
            start_direct(j)

    for copy in loads:
        copy.wait()

    def cols_of(b):
        return pl.ds(b * COLS, COLS)

    def scaled(c, _):
        for b in range(blocks):
            wide = q_ref[c, cols_of(b)].astype(jnp.float32) * scale
            high = wide.astype(jnp.bfloat16)
            qq_ref[c, cols_of(b), :size] = high
            qq_ref[c, cols_of(b), size:] = (wide - high.astype(jnp.float32)).astype(jnp.bfloat16)
        return 0

    lax.fori_loop(0, slots, scaled, 0)

    def score(c, b, keys, causal):
        n = keys.shape[0]
        s = lax.dot_general(
            jnp.concatenate([keys, keys], axis=1),
            qq_ref[c, cols_of(b)],
            (((1,), (1,)), ((), ())),
            preferred_element_type=jnp.float32,
        )
        if causal:
            key_at = lax.broadcasted_iota(jnp.int32, s.shape, 0)
            row_at = (lax.broadcasted_iota(jnp.int32, s.shape, 1) + b * COLS) // heads
            s = jnp.where(key_at <= row_at, s, NEG)
        s_ref[:n, cols_of(b)] = s
        top_ref[:, cols_of(b)] = jnp.max(s.reshape(n // 8, 8, COLS), axis=0)

    def weigh(c, b, n):
        cols = cols_of(b)
        old = m_ref[c, :, cols]
        peak = jnp.maximum(old, jnp.max(top_ref[:, cols], axis=0, keepdims=True))
        m_ref[c, :, cols] = peak
        alpha_ref[:, cols] = jnp.exp2(old - peak)
        p_ref[:n, cols] = jnp.exp2(s_ref[:n, cols] - peak).astype(jnp.bfloat16)

    def gather(c, b, values):
        cols = cols_of(b)
        acc_ref[c, :, cols] = acc_ref[c, :, cols] * alpha_ref[:, cols] + jnp.dot(
            values, p_ref[:, cols], preferred_element_type=jnp.float32
        )

    def keep_columns(values):
        n = values.shape[0]
        vt_ref[:size, :n] = values.T
        if n < most:
            vt_ref[:size, n:] = jnp.zeros((size, most - n), jnp.bfloat16)
        vt_ref[size:, :] = (lax.broadcasted_iota(jnp.int32, (EXTRA, most), 1) < n).astype(jnp.bfloat16)

    def stages(c, n, values, scored, keys, causal):
        earlier = vt_ref[...]
        for b in range(blocks):
            gather(jnp.bitwise_and(c + slots - 1, slots - 1), b, earlier)
            weigh(c, b, n)
            if keys is not None:
                score(scored, b, keys, causal)
        keep_columns(values)

    def zero(c, _):
        acc_ref[c] = jnp.zeros(acc_ref.shape[1:], jnp.float32)
        m_ref[c] = jnp.full(m_ref.shape[1:], NEG, jnp.float32)
        return 0

    lax.fori_loop(0, slots, zero, 0)
    vt_ref[...] = jnp.zeros(vt_ref.shape, jnp.bfloat16)
    p_ref[...] = jnp.zeros(p_ref.shape, jnp.bfloat16)
    alpha_ref[...] = jnp.ones(alpha_ref.shape, jnp.float32)

    group = lax.broadcasted_iota(jnp.int32, member_ref.shape, 0) // heads
    member_ref[...] = (group == lax.broadcasted_iota(jnp.int32, member_ref.shape, 1)).astype(jnp.bfloat16)
    to_row = lax.broadcasted_iota(jnp.int32, (2 * heads, 2 * heads), 0)
    from_row = lax.broadcasted_iota(jnp.int32, (2 * heads, 2 * heads), 1)
    order = (from_row == lax.rem(to_row, heads) * 2 + to_row // heads).astype(jnp.bfloat16)
    w_ref[...] = jnp.dot(order, w_ref[...], preferred_element_type=jnp.float32).astype(jnp.bfloat16)

    for b in range(blocks):
        score(0, b, ck_ref[0], True)

    def own_step(c, _):
        stages(c, ck_ref.shape[1], cv_ref[c], c + 1, ck_ref[c + 1], True)
        return 0

    lax.fori_loop(0, slots - 1, own_step, 0)

    def distance(c):
        return jnp.bitwise_and(dp - parent_ref[0, c], 3)

    def arrive(j):
        own_whole(j).wait()
        wait_slot(j, 1)
        wait_slot(j, 3)

    def cross_over(j):
        end = slots - 1
        values = cv_ref[end] if j == 0 else bufs[j - 1][distance(end), 1]
        keys = None if j == chunks else bufs[j][distance(0), 0]
        stages(end, values.shape[0], values, 0, keys, False)

    def compute(j):
        arrive(j)
        cross_over(j)

        def one(c, _):
            stages(c, sizes[j], bufs[j][distance(c), 1], c + 1, bufs[j][distance(c + 1), 0], False)
            return 0

        lax.fori_loop(0, slots - 1, one, 0)

    for j in range(chunks):
        wait_slot(j, 2)
        forward(j)
        if j + AHEAD < chunks:
            pl.when(jnp.logical_not(eager))(functools.partial(start_direct, j + AHEAD))

        @pl.when(core == 1)
        def _():
            for k in RELAY[j]:
                pass_on(k)

        if j >= 2:
            settle(j - 2)
        if j >= 1:
            compute(j - 1)
    compute(chunks - 1)
    cross_over(chunks)
    for b in range(blocks):
        gather(slots - 1, b, vt_ref[...])

    weight = w_ref[...]
    head_at = lax.broadcasted_iota(jnp.int32, (heads, rows), 1) % heads
    same = head_at == lax.broadcasted_iota(jnp.int32, (heads, rows), 0)

    def last(c, _):
        inverse = jnp.where(c < count_ref[0], 1.0 / acc_ref[c, size : size + 1], 0.0)
        done = (acc_ref[c, :size] * inverse).astype(jnp.bfloat16)
        done_ref[c] = done
        both = jnp.dot(weight, done, preferred_element_type=jnp.float32)
        for k in (0, 1):
            z_ref[c, k] = jnp.sum(jnp.where(same, both[k * heads : (k + 1) * heads], 0.0), axis=0, keepdims=True)
        return 0

    lax.fori_loop(0, slots, last, 0)

    lanes = z_ref[...].reshape(2 * slots, rows)
    high = lanes.astype(jnp.bfloat16)
    rest = lanes - high.astype(jnp.float32)
    middle = rest.astype(jnp.bfloat16)
    low = (rest - middle.astype(jnp.float32)).astype(jnp.bfloat16)
    sums = jnp.dot(jnp.concatenate([high, middle, low], axis=0), member_ref[...], preferred_element_type=jnp.float32)
    part_ref[...] = sums[: 2 * slots] + sums[2 * slots : 4 * slots] + sums[4 * slots :]

    def to_peer(step):
        return pltpu.make_async_remote_copy(
            src_ref=part_ref,
            dst_ref=gather_ref.at[step - 1],
            send_sem=y_send.at[step - 1],
            recv_sem=y_recv.at[step - 1],
            device_id=(dp, lax.rem(mp + step, n_mp)),
            device_id_type=MESH,
        )

    for step in range(1, n_mp):
        to_peer(step).start()

    def store(c, _):
        att_ref[c] = done_ref[c].T
        return 0

    lax.fori_loop(0, slots, store, 0)
    for j in range(max(chunks - 2, 0), chunks):
        settle(j)
    total = part_ref[...]
    for step in range(1, n_mp):
        to_peer(step).wait_recv()
        total = total + gather_ref[step - 1]
    logit_ref[...] = total
    for step in range(1, n_mp):
        to_peer(step).wait_send()


def solution(mesh):
    n_dp, n_mp = mesh.shape["dp"], mesh.shape["mp"]

    def step(queries, keys, values, prefix_keys, prefix_values, count, parent, weight):
        _, slots, steps, heads, size = queries.shape
        prefix = prefix_keys.shape[1]
        rows = steps * heads
        sizes = [prefix * n // sum(SIZES) for n in SIZES]
        chunks, most = len(sizes), max(sizes)
        bf16, f32 = jnp.bfloat16, jnp.float32
        dma = pltpu.SemaphoreType.DMA
        attended, logits = pl.pallas_call(
            functools.partial(kernel, n_dp, n_mp),
            out_shape=(
                jax.ShapeDtypeStruct((slots, rows, size), bf16),
                jax.ShapeDtypeStruct((2 * slots, steps), f32),
            ),
            in_specs=[pl.BlockSpec(memory_space=pltpu.HBM)] * 8,
            out_specs=(pl.BlockSpec(memory_space=pltpu.VMEM),) * 2,
            scratch_shapes=[pltpu.VMEM((4, 2, n, size), bf16) for n in sizes]
            + [pltpu.VMEM((2, n, size), bf16) for n in sizes]
            + [
                pltpu.VMEM((slots, rows, size), bf16),
                pltpu.VMEM((slots, steps, size), bf16),
                pltpu.VMEM((slots, steps, size), bf16),
                pltpu.VMEM((2 * heads, size), bf16),
                pltpu.SMEM((1,), jnp.int32),
                pltpu.SMEM((1, slots), jnp.int32),
                pltpu.VMEM((slots, size + EXTRA, rows), f32),
                pltpu.VMEM((slots, 1, rows), f32),
                pltpu.VMEM((slots, rows, 2 * size), bf16),
                pltpu.VMEM((2 * slots, steps), f32),
                pltpu.VMEM((max(n_mp - 1, 1), 2 * slots, steps), f32),
                pltpu.VMEM((slots, 2, 1, rows), f32),
                pltpu.VMEM((size + EXTRA, most), bf16),
                pltpu.VMEM((rows, steps), bf16),
                pltpu.VMEM((slots, size, rows), bf16),
            ]
            + [
                pltpu.VMEM((most, rows), f32),
                pltpu.VMEM((8, rows), f32),
                pltpu.VMEM((most, rows), bf16),
                pltpu.VMEM((1, rows), f32),
            ]
            + [dma((6,)), dma((chunks,)), dma((3, chunks))]
            + [dma((chunks,))] * 6
            + [dma((max(n_mp - 1, 1),))] * 2,
            compiler_params=pltpu.CompilerParams(
                collective_id=0, has_side_effects=True, vmem_limit_bytes=VMEM_LIMIT
            ),
            name="prefix_attention",
        )(
            queries.reshape(slots, rows, size),
            keys.reshape(slots, steps, size),
            values.reshape(slots, steps, size),
            prefix_keys.reshape(prefix, size),
            prefix_values.reshape(prefix, size),
            jnp.transpose(weight, (0, 2, 1)).reshape(2 * heads, size),
            count,
            parent,
        )
        attended = attended.reshape(1, slots, steps, heads, size)
        return attended, jnp.transpose(logits.reshape(slots, 2, steps), (0, 2, 1))[None]

    return jax.shard_map(
        step,
        mesh=mesh,
        in_specs=(
            P("dp", None, None, "mp", None),
            P("dp", None, None, "mp", None),
            P("dp", None, None, "mp", None),
            P("dp", None, "mp", None),
            P("dp", None, "mp", None),
            P("dp"),
            P("dp", None),
            P("mp", None, None),
        ),
        out_specs=(P("dp", None, None, "mp", None), P("dp", None, None, None)),
        check_vma=False,
    )
```

```python
import functools

import jax
import jax.numpy as jnp
from jax import lax
from jax.experimental import pallas as pl
from jax.experimental.pallas import tpu as pltpu
from jax.sharding import PartitionSpec as P

MESH = pl.DeviceIdType.MESH
SIZES = (8, 8, 8, 8, 8, 8, 8, 4, 4)
DETOUR = ()
RELAY = ((0, 1, 2), (3, 4, 5), (6, 7, 8), (), (), (), (), (), ())
AHEAD = 4
COLS = 256
EXTRA = 16
RING = 8
LOG2E = 1.4426950408889634
NEG = -1.0e30
VMEM_LIMIT = 60 * 1024 * 1024


def kernel(n_dp, n_mp, q_hbm, ck_hbm, cv_hbm, pk_hbm, pv_hbm, w_hbm, count_hbm, parent_hbm, att_hbm, logit_ref, *scratch):
    scratch = list(scratch)

    def take(n):
        taken, scratch[:n] = scratch[:n], []
        return taken

    chunks = len(SIZES)
    bufs, relays = take(chunks), take(chunks)
    q_ref, ck_ref, cv_ref, w_ref, count_ref, parent_ref = take(6)
    acc_ref, m_ref, qq_ref, part_ref, gather_ref, z_ref, vt_ref, member_ref, done_ref = take(9)
    s_ref, top_ref, p_ref, alpha_ref = take(4)
    in_sem, own_sem, recv_sem, z_sem, d2d_sem, fwd_sem, out_sem, relay_sem, pass_sem, done_sem, y_send, y_recv = scratch

    slots, rows, size = q_ref.shape
    prefix = pk_hbm.shape[0]
    heads = w_ref.shape[0] // 2
    blocks = rows // COLS
    scale = LOG2E * size**-0.5
    sizes = [prefix * n // sum(SIZES) for n in SIZES]
    most = max(sizes)
    starts = [sum(sizes[:j]) for j in range(chunks)]

    dp = lax.axis_index("dp")
    mp = lax.axis_index("mp")
    core = lax.rem(dp, 2)
    z = lax.rem(dp // 2, RING)
    plane = dp // (2 * RING)
    planes = n_dp // (2 * RING)

    def at(x, chip, which):
        return (lax.rem(x + planes, planes) * RING + chip) * 2 + which

    mate = dp + 1 - 2 * core
    ahead = lax.rem(dp + 2, n_dp)
    behind = lax.rem(dp + n_dp - 2, n_dp)
    cross = lax.rem(dp + n_dp + 2 * core - 1, n_dp)
    via = at(plane + (z + 2) // RING, lax.rem(z + RING - 3, RING), 1)
    served = lax.rem(z + 3, RING)
    served_from = at(plane - (served + 2) // RING, served, 1)
    drop = at(plane, lax.rem(served + 2, RING), 0)
    brought = at(plane, lax.rem(z + 3, RING), 1)

    sources = (pk_hbm, pv_hbm)

    def part(j):
        return pl.ds(starts[j], sizes[j])

    def own(j, kind):
        return pltpu.make_async_copy(sources[kind].at[part(j)], bufs[j].at[0, kind], own_sem.at[j])

    def own_whole(j):
        return pltpu.make_async_copy(bufs[j].at[1], bufs[j].at[0], own_sem.at[j])

    loads = [
        pltpu.make_async_copy(src, dst, in_sem.at[k])
        for k, (src, dst) in enumerate(
            (
                (parent_hbm, parent_ref),
                (count_hbm, count_ref),
                (q_hbm, q_ref),
                (ck_hbm, ck_ref),
                (cv_hbm, cv_ref),
                (w_hbm, w_ref),
            )
        )
    ]

    barrier = pltpu.get_barrier_semaphore()

    def greet(*others):
        for other in others:
            pl.semaphore_signal(barrier, inc=1, device_id=(other, mp), device_id_type=MESH)

    greet(mate, behind)
    for step in range(1, n_mp):
        pl.semaphore_signal(barrier, inc=1, device_id=(dp, lax.rem(mp + step, n_mp)), device_id_type=MESH)

    def ring_used(owner):
        return lax.rem(owner + 2, RING) == 0 if not DETOUR else owner >= 0

    relayed_to = lax.rem(z + RING - 2, RING)

    @pl.when(core == 0)
    def _():
        greet(cross)
        pl.when(ring_used(relayed_to))(lambda: greet(brought))

    @pl.when(core == 1)
    def _():
        pl.when(ring_used(served))(lambda: greet(served_from))

    for copy in loads:
        copy.start()
    for j in range(chunks):
        for kind in (0, 1):
            own(j, kind).start()
    sends_via, sends_on = (core * ring_used(owner).astype(jnp.int32) for owner in (z, served))
    pl.semaphore_wait(barrier, 2 + n_mp - 1 + core + sends_via + sends_on)

    def remote(src, dst, send, recv, target):
        return pltpu.make_async_remote_copy(
            src_ref=src, dst_ref=dst, send_sem=send, recv_sem=recv, device_id=(target, mp), device_id_type=MESH
        )

    def to_ahead(j, kind):
        return remote(sources[kind].at[part(j)], bufs[j].at[2, kind], z_sem.at[j], recv_sem.at[1, j], ahead)

    def own_to_mate(j, kind):
        return remote(sources[kind].at[part(j)], bufs[j].at[1, kind], d2d_sem.at[j], recv_sem.at[0, j], mate)

    def own_to_via(j, kind):
        return remote(sources[kind].at[part(j)], relays[j].at[kind], out_sem.at[j], relay_sem.at[j], via)

    def two_to_mate(j, slot):
        return remote(bufs[j].at[2], bufs[j].at[slot], fwd_sem.at[j], recv_sem.at[slot - 1, j], mate)

    def two_to_next(j):
        return remote(bufs[j].at[2], bufs[j].at[3], d2d_sem.at[j], recv_sem.at[2, j], cross)

    def relay_on(j):
        return remote(relays[j], bufs[j].at[3], pass_sem.at[j], recv_sem.at[2, j], drop)

    def whole(j, send, recv):
        return remote(bufs[j].at[2], bufs[j].at[1], send, recv, mate)

    def wait_slot(j, slot):
        whole(j, z_sem.at[j], recv_sem.at[slot - 1, j]).wait_recv()

    def wait_sent(j, sem):
        whole(j, sem.at[j], recv_sem.at[0, j]).wait_send()

    def on_ring(j, owner, do):
        if j in DETOUR:
            do()
        else:
            pl.when(lax.rem(owner + 2, RING) == 0)(do)

    def off_ring(j, owner, do):
        if j not in DETOUR:
            pl.when(lax.rem(owner + 2, RING) != 0)(do)

    def start_direct(j):
        for kind in (0, 1):
            to_ahead(j, kind).start()

        @pl.when(core == 0)
        def _():
            for kind in (0, 1):
                own_to_mate(j, kind).start()

    def start_detour(j):
        def do():
            for kind in (0, 1):
                own_to_via(j, kind).start()

        on_ring(j, z, do)

    def pass_on(j):
        def do():
            remote(relays[j], relays[j], out_sem.at[j], relay_sem.at[j], via).wait_recv()
            relay_on(j).start()

        on_ring(j, served, do)

    def forward(j):
        @pl.when(core == 0)
        def _():
            two_to_mate(j, 3).start()

        @pl.when(core == 1)
        def _():
            two_to_mate(j, 1).start()
            off_ring(j, lax.rem(z + RING - 1, RING), lambda: two_to_next(j).start())

    def settle(j):
        wait_sent(j, z_sem)
        wait_sent(j, fwd_sem)

        @pl.when(core == 0)
        def _():
            wait_sent(j, d2d_sem)

        @pl.when(core == 1)
        def _():
            off_ring(j, lax.rem(z + RING - 1, RING), lambda: wait_sent(j, d2d_sem))
            on_ring(j, z, lambda: wait_sent(j, out_sem))
            on_ring(j, served, lambda: wait_sent(j, pass_sem))

    start_direct(0)

    @pl.when(core == 1)
    def _():
        for j in range(chunks):
            start_detour(j)

    for j in range(1, AHEAD):
        start_direct(j)
    eager = lax.rem(z + 1, RING) <= 1

    @pl.when(eager)
    def _():
        for j in range(AHEAD, chunks):
            start_direct(j)

    for copy in loads:
        copy.wait()

    def cols_of(b):
        return pl.ds(b * COLS, COLS)

    def scaled(c, _):
        for b in range(blocks):
            wide = q_ref[c, cols_of(b)].astype(jnp.float32) * scale
            high = wide.astype(jnp.bfloat16)
            qq_ref[c, cols_of(b), :size] = high
            qq_ref[c, cols_of(b), size:] = (wide - high.astype(jnp.float32)).astype(jnp.bfloat16)
        return 0

    lax.fori_loop(0, slots, scaled, 0)

    def score(c, b, keys, causal):
        n = keys.shape[0]
        s = lax.dot_general(
            jnp.concatenate([keys, keys], axis=1),
            qq_ref[c, cols_of(b)],
            (((1,), (1,)), ((), ())),
            preferred_element_type=jnp.float32,
        )
        if causal:
            key_at = lax.broadcasted_iota(jnp.int32, s.shape, 0)
            row_at = (lax.broadcasted_iota(jnp.int32, s.shape, 1) + b * COLS) // heads
            s = jnp.where(key_at <= row_at, s, NEG)
        s_ref[:n, cols_of(b)] = s
        top_ref[:, cols_of(b)] = jnp.max(s.reshape(n // 8, 8, COLS), axis=0)

    def weigh(c, b, n):
        cols = cols_of(b)
        old = m_ref[c, :, cols]
        peak = jnp.maximum(old, jnp.max(top_ref[:, cols], axis=0, keepdims=True))
        m_ref[c, :, cols] = peak
        alpha_ref[:, cols] = jnp.exp2(old - peak)
        p_ref[:n, cols] = jnp.exp2(s_ref[:n, cols] - peak).astype(jnp.bfloat16)

    def gather(c, b, values):
        cols = cols_of(b)
        acc_ref[c, :, cols] = acc_ref[c, :, cols] * alpha_ref[:, cols] + jnp.dot(
            values, p_ref[:, cols], preferred_element_type=jnp.float32
        )

    def keep_columns(values):
        n = values.shape[0]
        vt_ref[:size, :n] = values.T
        if n < most:
            vt_ref[:size, n:] = jnp.zeros((size, most - n), jnp.bfloat16)
        vt_ref[size:, :] = (lax.broadcasted_iota(jnp.int32, (EXTRA, most), 1) < n).astype(jnp.bfloat16)

    def stages(c, n, values, scored, keys, causal):
        earlier = vt_ref[...]
        for b in range(blocks):
            gather((c + slots - 1) % slots, b, earlier)
            weigh(c, b, n)
            if keys is not None:
                score(scored, b, keys, causal)
        keep_columns(values)

    def zero(c, _):
        acc_ref[c] = jnp.zeros(acc_ref.shape[1:], jnp.float32)
        m_ref[c] = jnp.full(m_ref.shape[1:], NEG, jnp.float32)
        return 0

    lax.fori_loop(0, slots, zero, 0)
    vt_ref[...] = jnp.zeros(vt_ref.shape, jnp.bfloat16)
    p_ref[...] = jnp.zeros(p_ref.shape, jnp.bfloat16)
    alpha_ref[...] = jnp.ones(alpha_ref.shape, jnp.float32)

    group = lax.broadcasted_iota(jnp.int32, member_ref.shape, 0) // heads
    member_ref[...] = (group == lax.broadcasted_iota(jnp.int32, member_ref.shape, 1)).astype(jnp.bfloat16)
    to_row = lax.broadcasted_iota(jnp.int32, (2 * heads, 2 * heads), 0)
    from_row = lax.broadcasted_iota(jnp.int32, (2 * heads, 2 * heads), 1)
    order = (from_row == lax.rem(to_row, heads) * 2 + to_row // heads).astype(jnp.bfloat16)
    w_ref[...] = jnp.dot(order, w_ref[...], preferred_element_type=jnp.float32).astype(jnp.bfloat16)

    head_at = lax.broadcasted_iota(jnp.int32, (heads, rows), 1) % heads
    same = head_at == lax.broadcasted_iota(jnp.int32, (heads, rows), 0)

    def out(c):
        return pltpu.make_async_copy(done_ref.at[c], att_hbm.at[c], done_sem.at[c])

    def finish(c):
        inverse = jnp.where(c < count_ref[0], 1.0 / acc_ref[c, size : size + 1], 0.0)
        done = (acc_ref[c, :size] * inverse).astype(jnp.bfloat16)
        both = jnp.dot(w_ref[...], done, preferred_element_type=jnp.float32)
        for k in (0, 1):
            z_ref[c, k] = jnp.sum(jnp.where(same, both[k * heads : (k + 1) * heads], 0.0), axis=0, keepdims=True)
        done_ref[c] = done.T
        out(c).start()

    for b in range(blocks):
        score(0, b, ck_ref[0], True)

    for c in range(slots - 1):
        stages(c, ck_ref.shape[1], cv_ref[c], c + 1, ck_ref[c + 1], True)

    def distance(c):
        return jnp.bitwise_and(dp - parent_ref[0, c], 3)

    def arrive(j):
        own_whole(j).wait()
        wait_slot(j, 1)
        wait_slot(j, 3)

    def cross_over(j):
        end = slots - 1
        values = cv_ref[end] if j == 0 else bufs[j - 1][distance(end), 1]
        keys = None if j == chunks else bufs[j][distance(0), 0]
        stages(end, values.shape[0], values, 0, keys, False)

    def compute(j):
        arrive(j)
        cross_over(j)
        for c in range(slots - 1):
            stages(c, sizes[j], bufs[j][distance(c), 1], c + 1, bufs[j][distance(c + 1), 0], False)
            if j == chunks - 1 and c >= 1:
                finish(c - 1)

    for j in range(chunks):
        wait_slot(j, 2)
        forward(j)
        if j + AHEAD < chunks:
            pl.when(jnp.logical_not(eager))(functools.partial(start_direct, j + AHEAD))

        @pl.when(core == 1)
        def _():
            for k in RELAY[j]:
                pass_on(k)

        if j >= 2:
            settle(j - 2)
        if j >= 1:
            compute(j - 1)
    compute(chunks - 1)
    cross_over(chunks)
    finish(slots - 2)
    for b in range(blocks):
        gather(slots - 1, b, vt_ref[...])
    finish(slots - 1)

    lanes = z_ref[...].reshape(2 * slots, rows)
    high = lanes.astype(jnp.bfloat16)
    rest = lanes - high.astype(jnp.float32)
    middle = rest.astype(jnp.bfloat16)
    low = (rest - middle.astype(jnp.float32)).astype(jnp.bfloat16)
    sums = jnp.dot(jnp.concatenate([high, middle, low], axis=0), member_ref[...], preferred_element_type=jnp.float32)
    part_ref[...] = sums[: 2 * slots] + sums[2 * slots : 4 * slots] + sums[4 * slots :]

    def to_peer(step):
        return pltpu.make_async_remote_copy(
            src_ref=part_ref,
            dst_ref=gather_ref.at[step - 1],
            send_sem=y_send.at[step - 1],
            recv_sem=y_recv.at[step - 1],
            device_id=(dp, lax.rem(mp + step, n_mp)),
            device_id_type=MESH,
        )

    for step in range(1, n_mp):
        to_peer(step).start()

    for j in range(max(chunks - 2, 0), chunks):
        settle(j)
    for c in range(slots):
        out(c).wait()
    total = part_ref[...]
    for step in range(1, n_mp):
        to_peer(step).wait_recv()
        total = total + gather_ref[step - 1]
    logit_ref[...] = total
    for step in range(1, n_mp):
        to_peer(step).wait_send()


def solution(mesh):
    n_dp, n_mp = mesh.shape["dp"], mesh.shape["mp"]

    def step(queries, keys, values, prefix_keys, prefix_values, count, parent, weight):
        _, slots, steps, heads, size = queries.shape
        prefix = prefix_keys.shape[1]
        rows = steps * heads
        sizes = [prefix * n // sum(SIZES) for n in SIZES]
        chunks, most = len(sizes), max(sizes)
        bf16, f32 = jnp.bfloat16, jnp.float32
        dma = pltpu.SemaphoreType.DMA
        attended, logits = pl.pallas_call(
            functools.partial(kernel, n_dp, n_mp),
            out_shape=(
                jax.ShapeDtypeStruct((slots, rows, size), bf16),
                jax.ShapeDtypeStruct((2 * slots, steps), f32),
            ),
            in_specs=[pl.BlockSpec(memory_space=pltpu.HBM)] * 8,
            out_specs=(pl.BlockSpec(memory_space=pltpu.HBM), pl.BlockSpec(memory_space=pltpu.VMEM)),
            scratch_shapes=[pltpu.VMEM((4, 2, n, size), bf16) for n in sizes]
            + [pltpu.VMEM((2, n, size), bf16) for n in sizes]
            + [
                pltpu.VMEM((slots, rows, size), bf16),
                pltpu.VMEM((slots, steps, size), bf16),
                pltpu.VMEM((slots, steps, size), bf16),
                pltpu.VMEM((2 * heads, size), bf16),
                pltpu.SMEM((1,), jnp.int32),
                pltpu.SMEM((1, slots), jnp.int32),
                pltpu.VMEM((slots, size + EXTRA, rows), f32),
                pltpu.VMEM((slots, 1, rows), f32),
                pltpu.VMEM((slots, rows, 2 * size), bf16),
                pltpu.VMEM((2 * slots, steps), f32),
                pltpu.VMEM((max(n_mp - 1, 1), 2 * slots, steps), f32),
                pltpu.VMEM((slots, 2, 1, rows), f32),
                pltpu.VMEM((size + EXTRA, most), bf16),
                pltpu.VMEM((rows, steps), bf16),
                pltpu.VMEM((slots, rows, size), bf16),
            ]
            + [
                pltpu.VMEM((most, rows), f32),
                pltpu.VMEM((8, rows), f32),
                pltpu.VMEM((most, rows), bf16),
                pltpu.VMEM((1, rows), f32),
            ]
            + [dma((6,)), dma((chunks,)), dma((3, chunks))]
            + [dma((chunks,))] * 6
            + [dma((slots,))]
            + [dma((max(n_mp - 1, 1),))] * 2,
            compiler_params=pltpu.CompilerParams(
                collective_id=0, has_side_effects=True, vmem_limit_bytes=VMEM_LIMIT
            ),
            name="prefix_attention",
        )(
            queries.reshape(slots, rows, size),
            keys.reshape(slots, steps, size),
            values.reshape(slots, steps, size),
            prefix_keys.reshape(prefix, size),
            prefix_values.reshape(prefix, size),
            jnp.transpose(weight, (0, 2, 1)).reshape(2 * heads, size),
            count,
            parent,
        )
        attended = attended.reshape(1, slots, steps, heads, size)
        return attended, jnp.transpose(logits.reshape(slots, 2, steps), (0, 2, 1))[None]

    return jax.shard_map(
        step,
        mesh=mesh,
        in_specs=(
            P("dp", None, None, "mp", None),
            P("dp", None, None, "mp", None),
            P("dp", None, None, "mp", None),
            P("dp", None, "mp", None),
            P("dp", None, "mp", None),
            P("dp"),
            P("dp", None),
            P("mp", None, None),
        ),
        out_specs=(P("dp", None, None, "mp", None), P("dp", None, None, None)),
        check_vma=False,
    )
```

```python
import functools

import jax
import jax.numpy as jnp
from jax import lax
from jax.experimental import pallas as pl
from jax.experimental.pallas import tpu as pltpu
from jax.sharding import PartitionSpec as P

MESH = pl.DeviceIdType.MESH
SIZES = (8, 8, 8, 8, 8, 8, 8, 4, 4)
DETOUR = (7, 8)
RELAY = ((0, 1, 2), (3, 4, 5), (6,), (7, 8), (), (), (), (), ())
AHEAD = 4
EASE = 2
COLS = 256
EXTRA = 16
RING = 8
LOG2E = 1.4426950408889634
NEG = -1.0e30
VMEM_LIMIT = 60 * 1024 * 1024


def kernel(n_dp, n_mp, q_hbm, ck_hbm, cv_hbm, pk_hbm, pv_hbm, w_hbm, count_hbm, parent_hbm, att_hbm, logit_ref, *scratch):
    scratch = list(scratch)

    def take(n):
        taken, scratch[:n] = scratch[:n], []
        return taken

    chunks = len(SIZES)
    bufs, relays = take(chunks), take(chunks)
    q_ref, ck_ref, cv_ref, w_ref, count_ref, parent_ref = take(6)
    acc_ref, m_ref, qq_ref, part_ref, gather_ref, z_ref, vt_ref, member_ref, done_ref = take(9)
    s_ref, top_ref, p_ref, alpha_ref = take(4)
    in_sem, own_sem, recv_sem, z_sem, d2d_sem, fwd_sem, out_sem, relay_sem, pass_sem, done_sem, y_send, y_recv, via_ready, drop_ready = scratch

    slots, rows, size = q_ref.shape
    prefix = pk_hbm.shape[0]
    heads = w_ref.shape[0] // 2
    blocks = rows // COLS
    scale = LOG2E * size**-0.5
    sizes = [prefix * n // sum(SIZES) for n in SIZES]
    most = max(sizes)
    starts = [sum(sizes[:j]) for j in range(chunks)]

    dp = lax.axis_index("dp")
    mp = lax.axis_index("mp")
    core = lax.rem(dp, 2)
    z = lax.rem(dp // 2, RING)
    plane = dp // (2 * RING)
    planes = n_dp // (2 * RING)

    def at(x, chip, which):
        return (lax.rem(x + planes, planes) * RING + chip) * 2 + which

    mate = dp + 1 - 2 * core
    ahead = lax.rem(dp + 2, n_dp)
    behind = lax.rem(dp + n_dp - 2, n_dp)
    cross = lax.rem(dp + n_dp + 2 * core - 1, n_dp)
    via = at(plane + (z + 2) // RING, lax.rem(z + RING - 3, RING), 1)
    served = lax.rem(z + 3, RING)
    served_from = at(plane - (served + 2) // RING, served, 1)
    drop = at(plane, lax.rem(served + 2, RING), 0)
    brought = at(plane, lax.rem(z + 3, RING), 1)

    sources = (pk_hbm, pv_hbm)

    def part(j):
        return pl.ds(starts[j], sizes[j])

    def own(j, kind):
        return pltpu.make_async_copy(sources[kind].at[part(j)], bufs[j].at[0, kind], own_sem.at[j])

    def own_whole(j):
        return pltpu.make_async_copy(bufs[j].at[1], bufs[j].at[0], own_sem.at[j])

    loads = [
        pltpu.make_async_copy(src, dst, in_sem.at[k])
        for k, (src, dst) in enumerate(
            (
                (parent_hbm, parent_ref),
                (count_hbm, count_ref),
                (q_hbm, q_ref),
                (ck_hbm, ck_ref),
                (cv_hbm, cv_ref),
                (w_hbm, w_ref),
            )
        )
    ]

    barrier = pltpu.get_barrier_semaphore()

    def greet(*others):
        for other in others:
            pl.semaphore_signal(barrier, inc=1, device_id=(other, mp), device_id_type=MESH)

    greet(mate, behind)
    for step in range(1, n_mp):
        pl.semaphore_signal(barrier, inc=1, device_id=(dp, lax.rem(mp + step, n_mp)), device_id_type=MESH)

    def ring_used(owner):
        return lax.rem(owner + 2, RING) == 0 if not DETOUR else owner >= 0

    relayed_to = lax.rem(z + RING - 2, RING)
    sends_via = jnp.logical_and(core == 1, ring_used(z))
    passes_on = jnp.logical_and(core == 1, ring_used(served))
    is_brought = jnp.logical_and(core == 0, ring_used(relayed_to))
    via_late = z < 3
    served_early = z >= RING - 3
    drop_late = z < 3
    brought_early = z >= RING - 3
    no = jnp.logical_not

    def both(*conditions):
        return functools.reduce(jnp.logical_and, conditions)

    pl.when(core == 0)(lambda: greet(cross))
    pl.when(both(sends_via, via_late))(lambda: greet(via))
    pl.when(both(passes_on, no(served_early)))(lambda: greet(served_from))
    pl.when(both(passes_on, drop_late))(lambda: greet(drop))
    pl.when(both(is_brought, no(brought_early)))(lambda: greet(brought))

    for copy in loads:
        copy.start()
    for j in range(chunks):
        for kind in (0, 1):
            own(j, kind).start()
    waits_for = (
        both(sends_via, no(via_late)),
        both(passes_on, served_early),
        both(passes_on, no(drop_late)),
        both(is_brought, brought_early),
    )
    pl.semaphore_wait(barrier, 2 + n_mp - 1 + core + sum(w.astype(jnp.int32) for w in waits_for))

    def tell(other, sem):
        pl.semaphore_signal(sem, inc=1, device_id=(other, mp), device_id_type=MESH)

    pl.when(both(passes_on, served_early))(lambda: tell(served_from, via_ready))
    pl.when(both(is_brought, brought_early))(lambda: tell(brought, drop_ready))

    def remote(src, dst, send, recv, target):
        return pltpu.make_async_remote_copy(
            src_ref=src, dst_ref=dst, send_sem=send, recv_sem=recv, device_id=(target, mp), device_id_type=MESH
        )

    def to_ahead(j, kind):
        return remote(sources[kind].at[part(j)], bufs[j].at[2, kind], z_sem.at[j], recv_sem.at[1, j], ahead)

    def own_to_mate(j, kind):
        return remote(sources[kind].at[part(j)], bufs[j].at[1, kind], d2d_sem.at[j], recv_sem.at[0, j], mate)

    def own_to_via(j, kind):
        return remote(sources[kind].at[part(j)], relays[j].at[kind], out_sem.at[j], relay_sem.at[j], via)

    def two_to_mate(j, slot):
        return remote(bufs[j].at[2], bufs[j].at[slot], fwd_sem.at[j], recv_sem.at[slot - 1, j], mate)

    def two_to_next(j):
        return remote(bufs[j].at[2], bufs[j].at[3], d2d_sem.at[j], recv_sem.at[2, j], cross)

    def relay_on(j):
        return remote(relays[j], bufs[j].at[3], pass_sem.at[j], recv_sem.at[2, j], drop)

    def whole(j, send, recv):
        return remote(bufs[j].at[2], bufs[j].at[1], send, recv, mate)

    def wait_slot(j, slot):
        whole(j, z_sem.at[j], recv_sem.at[slot - 1, j]).wait_recv()

    def wait_sent(j, sem):
        whole(j, sem.at[j], recv_sem.at[0, j]).wait_send()

    def on_ring(j, owner, do):
        if j in DETOUR:
            do()
        else:
            pl.when(lax.rem(owner + 2, RING) == 0)(do)

    def off_ring(j, owner, do):
        if j not in DETOUR:
            pl.when(lax.rem(owner + 2, RING) != 0)(do)

    def start_direct(j):
        for kind in (0, 1):
            to_ahead(j, kind).start()

        @pl.when(core == 0)
        def _():
            for kind in (0, 1):
                own_to_mate(j, kind).start()

    def start_detour(j):
        def do():
            for kind in (0, 1):
                own_to_via(j, kind).start()

        on_ring(j, z, do)

    def pass_on(j):
        def do():
            remote(relays[j], relays[j], out_sem.at[j], relay_sem.at[j], via).wait_recv()
            relay_on(j).start()

        on_ring(j, served, do)

    def forward(j):
        @pl.when(core == 0)
        def _():
            two_to_mate(j, 3).start()

        @pl.when(core == 1)
        def _():
            off_ring(j, lax.rem(z + RING - 1, RING), lambda: two_to_next(j).start())
            two_to_mate(j, 1).start()

    def settle(j):
        wait_sent(j, z_sem)
        wait_sent(j, fwd_sem)

        @pl.when(core == 0)
        def _():
            wait_sent(j, d2d_sem)

        @pl.when(core == 1)
        def _():
            off_ring(j, lax.rem(z + RING - 1, RING), lambda: wait_sent(j, d2d_sem))
            on_ring(j, z, lambda: wait_sent(j, out_sem))
            on_ring(j, served, lambda: wait_sent(j, pass_sem))

    start_direct(0)

    def start_detours():
        for j in range(chunks):
            start_detour(j)

    pl.when(both(sends_via, no(via_late)))(start_detours)

    for j in range(1, AHEAD):
        start_direct(j)
    most_extra = chunks - AHEAD
    extra = jnp.where(z == RING - 1, most_extra, jnp.maximum(most_extra - EASE * z, 0))
    for j in range(AHEAD, chunks):
        pl.when(extra > j - AHEAD)(functools.partial(start_direct, j))

    for copy in loads:
        copy.wait()

    def cols_of(b):
        return pl.ds(b * COLS, COLS)

    def scaled(c, _):
        for b in range(blocks):
            wide = q_ref[c, cols_of(b)].astype(jnp.float32) * scale
            high = wide.astype(jnp.bfloat16)
            qq_ref[c, cols_of(b), :size] = high
            qq_ref[c, cols_of(b), size:] = (wide - high.astype(jnp.float32)).astype(jnp.bfloat16)
        return 0

    lax.fori_loop(0, slots, scaled, 0)

    def score(c, b, keys, causal):
        n = keys.shape[0]
        s = lax.dot_general(
            jnp.concatenate([keys, keys], axis=1),
            qq_ref[c, cols_of(b)],
            (((1,), (1,)), ((), ())),
            preferred_element_type=jnp.float32,
        )
        if causal:
            key_at = lax.broadcasted_iota(jnp.int32, s.shape, 0)
            row_at = (lax.broadcasted_iota(jnp.int32, s.shape, 1) + b * COLS) // heads
            s = jnp.where(key_at <= row_at, s, NEG)
        s_ref[:n, cols_of(b)] = s
        top_ref[:, cols_of(b)] = jnp.max(s.reshape(n // 8, 8, COLS), axis=0)

    def weigh(c, b, n):
        cols = cols_of(b)
        old = m_ref[c, :, cols]
        peak = jnp.maximum(old, jnp.max(top_ref[:, cols], axis=0, keepdims=True))
        m_ref[c, :, cols] = peak
        alpha_ref[:, cols] = jnp.exp2(old - peak)
        p_ref[:n, cols] = jnp.exp2(s_ref[:n, cols] - peak).astype(jnp.bfloat16)

    def gather(c, b, n):
        cols = cols_of(b)
        acc_ref[c, :, cols] = acc_ref[c, :, cols] * alpha_ref[:, cols] + jnp.dot(
            vt_ref[:, :n], p_ref[:n, cols], preferred_element_type=jnp.float32
        )

    def keep_columns(values):
        vt_ref[:size, : values.shape[0]] = values.T

    def stages(c, n, before, values, scored, keys, causal):
        for b in range(blocks):
            if before:
                gather((c + slots - 1) % slots, b, before)
            weigh(c, b, n)
            if keys is not None:
                score(scored, b, keys, causal)
        keep_columns(values)

    def zero(c, _):
        acc_ref[c] = jnp.zeros(acc_ref.shape[1:], jnp.float32)
        m_ref[c] = jnp.full(m_ref.shape[1:], NEG, jnp.float32)
        return 0

    lax.fori_loop(0, slots, zero, 0)
    vt_ref[size:, :] = jnp.ones((EXTRA, most), jnp.bfloat16)

    group = lax.broadcasted_iota(jnp.int32, member_ref.shape, 0) // heads
    member_ref[...] = (group == lax.broadcasted_iota(jnp.int32, member_ref.shape, 1)).astype(jnp.bfloat16)
    to_row = lax.broadcasted_iota(jnp.int32, (2 * heads, 2 * heads), 0)
    from_row = lax.broadcasted_iota(jnp.int32, (2 * heads, 2 * heads), 1)
    order = (from_row == lax.rem(to_row, heads) * 2 + to_row // heads).astype(jnp.bfloat16)
    w_ref[...] = jnp.dot(order, w_ref[...], preferred_element_type=jnp.float32).astype(jnp.bfloat16)

    head_at = lax.broadcasted_iota(jnp.int32, (heads, rows), 1) % heads
    same = head_at == lax.broadcasted_iota(jnp.int32, (heads, rows), 0)

    def out(c):
        return pltpu.make_async_copy(done_ref.at[c], att_hbm.at[c], done_sem.at[c])

    def finish(c):
        inverse = jnp.where(c < count_ref[0], 1.0 / acc_ref[c, size : size + 1], 0.0)
        done = (acc_ref[c, :size] * inverse).astype(jnp.bfloat16)
        both = jnp.dot(w_ref[...], done, preferred_element_type=jnp.float32)
        for k in (0, 1):
            z_ref[c, k] = jnp.sum(jnp.where(same, both[k * heads : (k + 1) * heads], 0.0), axis=0, keepdims=True)
        done_ref[c] = done.T
        out(c).start()

    for b in range(blocks):
        score(0, b, ck_ref[0], True)

    for c in range(slots - 1):
        stages(c, ck_ref.shape[1], ck_ref.shape[1] if c else 0, cv_ref[c], c + 1, ck_ref[c + 1], True)

    def distance(c):
        return jnp.bitwise_and(dp - parent_ref[0, c], 3)

    def arrive(j):
        own_whole(j).wait()
        wait_slot(j, 1)
        wait_slot(j, 3)

    def cross_over(j):
        end = slots - 1
        values = cv_ref[end] if j == 0 else bufs[j - 1][distance(end), 1]
        keys = None if j == chunks else bufs[j][distance(0), 0]
        stages(end, values.shape[0], values.shape[0], values, 0, keys, False)

    def compute(j):
        arrive(j)
        cross_over(j)
        for c in range(slots - 1):
            earlier = sizes[j] if c else sizes[j - 1] if j else ck_ref.shape[1]
            stages(c, sizes[j], earlier, bufs[j][distance(c), 1], c + 1, bufs[j][distance(c + 1), 0], False)
            if j == chunks - 1 and c >= 1:
                finish(c - 1)

    for j in range(chunks):
        wait_slot(j, 2)
        forward(j)
        for e in range(most_extra - j):
            pl.when(extra == e)(functools.partial(start_direct, j + AHEAD + e))

        if j == 0:

            @pl.when(both(sends_via, via_late))
            def _():
                pl.semaphore_wait(via_ready, 1)
                start_detours()

            @pl.when(both(passes_on, drop_late))
            def _():
                pl.semaphore_wait(drop_ready, 1)

        @pl.when(core == 1)
        def _():
            for k in RELAY[j]:
                pass_on(k)

        if j >= 2:
            settle(j - 2)
        if j >= 1:
            compute(j - 1)
    compute(chunks - 1)
    cross_over(chunks)
    finish(slots - 2)
    for b in range(blocks):
        gather(slots - 1, b, sizes[-1])
    finish(slots - 1)

    lanes = z_ref[...].reshape(2 * slots, rows)
    high = lanes.astype(jnp.bfloat16)
    rest = lanes - high.astype(jnp.float32)
    middle = rest.astype(jnp.bfloat16)
    low = (rest - middle.astype(jnp.float32)).astype(jnp.bfloat16)
    sums = jnp.dot(jnp.concatenate([high, middle, low], axis=0), member_ref[...], preferred_element_type=jnp.float32)
    part_ref[...] = sums[: 2 * slots] + sums[2 * slots : 4 * slots] + sums[4 * slots :]

    def to_peer(step):
        return pltpu.make_async_remote_copy(
            src_ref=part_ref,
            dst_ref=gather_ref.at[step - 1],
            send_sem=y_send.at[step - 1],
            recv_sem=y_recv.at[step - 1],
            device_id=(dp, lax.rem(mp + step, n_mp)),
            device_id_type=MESH,
        )

    for step in sorted(range(1, n_mp), key=lambda step: abs(2 * step - n_mp)):
        to_peer(step).start()

    for j in range(max(chunks - 2, 0), chunks):
        settle(j)
    for c in range(slots):
        out(c).wait()
    total = part_ref[...]
    for step in range(1, n_mp):
        to_peer(step).wait_recv()
        total = total + gather_ref[step - 1]
    logit_ref[...] = total
    for step in range(1, n_mp):
        to_peer(step).wait_send()


def place(att_in, logit_in, att_out, logit_out, att_ref, logit_ref, in_sem, out_sem):
    slots = att_in.shape[0]
    pieces = [(logit_in, logit_ref, logit_out)]
    pieces += [(att_in.at[c], att_ref.at[c], att_out.at[c]) for c in range(slots)]
    loads = [pltpu.make_async_copy(src, held, in_sem.at[k]) for k, (src, held, _) in enumerate(pieces)]
    stores = [pltpu.make_async_copy(held, dst, out_sem.at[k]) for k, (_, held, dst) in enumerate(pieces)]
    for load in loads:
        load.start()
    for load, store in zip(loads, stores):
        load.wait()
        store.start()
    for store in stores:
        store.wait()


def solution(mesh):
    n_dp, n_mp = mesh.shape["dp"], mesh.shape["mp"]

    def step(queries, keys, values, prefix_keys, prefix_values, count, parent, weight):
        _, slots, steps, heads, size = queries.shape
        prefix = prefix_keys.shape[1]
        rows = steps * heads
        sizes = [prefix * n // sum(SIZES) for n in SIZES]
        chunks, most = len(sizes), max(sizes)
        bf16, f32 = jnp.bfloat16, jnp.float32
        dma = pltpu.SemaphoreType.DMA
        attended, logits = pl.pallas_call(
            functools.partial(kernel, n_dp, n_mp),
            out_shape=(
                jax.ShapeDtypeStruct((slots, rows, size), bf16),
                jax.ShapeDtypeStruct((2 * slots, steps), f32),
            ),
            in_specs=[pl.BlockSpec(memory_space=pltpu.HBM)] * 8,
            out_specs=(pl.BlockSpec(memory_space=pltpu.HBM), pl.BlockSpec(memory_space=pltpu.VMEM)),
            scratch_shapes=[pltpu.VMEM((4, 2, n, size), bf16) for n in sizes]
            + [pltpu.VMEM((2, n, size), bf16) for n in sizes]
            + [
                pltpu.VMEM((slots, rows, size), bf16),
                pltpu.VMEM((slots, steps, size), bf16),
                pltpu.VMEM((slots, steps, size), bf16),
                pltpu.VMEM((2 * heads, size), bf16),
                pltpu.SMEM((1,), jnp.int32),
                pltpu.SMEM((1, slots), jnp.int32),
                pltpu.VMEM((slots, size + EXTRA, rows), f32),
                pltpu.VMEM((slots, 1, rows), f32),
                pltpu.VMEM((slots, rows, 2 * size), bf16),
                pltpu.VMEM((2 * slots, steps), f32),
                pltpu.VMEM((max(n_mp - 1, 1), 2 * slots, steps), f32),
                pltpu.VMEM((slots, 2, 1, rows), f32),
                pltpu.VMEM((size + EXTRA, most), bf16),
                pltpu.VMEM((rows, steps), bf16),
                pltpu.VMEM((slots, rows, size), bf16),
            ]
            + [
                pltpu.VMEM((most, rows), f32),
                pltpu.VMEM((8, rows), f32),
                pltpu.VMEM((most, rows), bf16),
                pltpu.VMEM((1, rows), f32),
            ]
            + [dma((6,)), dma((chunks,)), dma((3, chunks))]
            + [dma((chunks,))] * 6
            + [dma((slots,))]
            + [dma((max(n_mp - 1, 1),))] * 2
            + [pltpu.SemaphoreType.REGULAR] * 2,
            compiler_params=pltpu.CompilerParams(
                collective_id=0, has_side_effects=True, vmem_limit_bytes=VMEM_LIMIT
            ),
            name="prefix_attention",
        )(
            queries.reshape(slots, rows, size),
            keys.reshape(slots, steps, size),
            values.reshape(slots, steps, size),
            prefix_keys.reshape(prefix, size),
            prefix_values.reshape(prefix, size),
            jnp.transpose(weight, (0, 2, 1)).reshape(2 * heads, size),
            count,
            parent,
        )
        hbm = pl.BlockSpec(memory_space=pltpu.HBM)
        attended, logits = pl.pallas_call(
            place,
            out_shape=(
                jax.ShapeDtypeStruct((slots, rows, size), bf16),
                jax.ShapeDtypeStruct((2 * slots, steps), f32),
            ),
            in_specs=[hbm] * 2,
            out_specs=(hbm, hbm),
            scratch_shapes=[
                pltpu.VMEM((slots, rows, size), bf16),
                pltpu.VMEM((2 * slots, steps), f32),
                dma((slots + 1,)),
                dma((slots + 1,)),
            ],
            compiler_params=pltpu.CompilerParams(vmem_limit_bytes=VMEM_LIMIT),
            name="place",
        )(attended, logits)
        attended = attended.reshape(1, slots, steps, heads, size)
        return attended, jnp.transpose(logits.reshape(slots, 2, steps), (0, 2, 1))[None]

    return jax.shard_map(
        step,
        mesh=mesh,
        in_specs=(
            P("dp", None, None, "mp", None),
            P("dp", None, None, "mp", None),
            P("dp", None, None, "mp", None),
            P("dp", None, "mp", None),
            P("dp", None, "mp", None),
            P("dp"),
            P("dp", None),
            P("mp", None, None),
        ),
        out_specs=(P("dp", None, None, "mp", None), P("dp", None, None, None)),
        check_vma=False,
    )
```

```python
import functools

import jax
import jax.numpy as jnp
from jax import lax
from jax.experimental import pallas as pl
from jax.experimental.pallas import tpu as pltpu
from jax.sharding import PartitionSpec as P

MESH = pl.DeviceIdType.MESH
SIZES = (8, 8, 8, 8, 8, 8, 8, 4, 4)
DETOUR = (6, 7, 8)
RELAY = ((0, 1, 2), (3, 4, 5), (), (), (6, 7, 8), (), (), (), ())
AHEAD = 4
EASE = 2
COLS = 256
EXTRA = 16
RING = 8
LOG2E = 1.4426950408889634
NEG = -1.0e30
VMEM_LIMIT = 60 * 1024 * 1024


def kernel(n_dp, n_mp, q_hbm, ck_hbm, cv_hbm, pk_hbm, pv_hbm, w_hbm, count_hbm, parent_hbm, att_hbm, logit_ref, *scratch):
    scratch = list(scratch)

    def take(n):
        taken, scratch[:n] = scratch[:n], []
        return taken

    chunks = len(SIZES)
    bufs, relays = take(chunks), take(chunks)
    q_ref, ck_ref, cv_ref, w_ref, count_ref, parent_ref = take(6)
    acc_ref, m_ref, qq_ref, part_ref, gather_ref, z_ref, vt_ref, member_ref, done_ref = take(9)
    s_ref, top_ref, p_ref, alpha_ref = take(4)
    in_sem, own_sem, recv_sem, z_sem, d2d_sem, fwd_sem, out_sem, relay_sem, pass_sem, done_sem, y_send, y_recv, via_ready, drop_ready = scratch

    slots, rows, size = q_ref.shape
    prefix = pk_hbm.shape[0]
    heads = w_ref.shape[0] // 2
    blocks = rows // COLS
    scale = LOG2E * size**-0.5
    sizes = [prefix * n // sum(SIZES) for n in SIZES]
    most = max(sizes)
    starts = [sum(sizes[:j]) for j in range(chunks)]

    dp = lax.axis_index("dp")
    mp = lax.axis_index("mp")
    core = lax.rem(dp, 2)
    z = lax.rem(dp // 2, RING)
    plane = dp // (2 * RING)
    planes = n_dp // (2 * RING)

    def at(x, chip, which):
        return (lax.rem(x + planes, planes) * RING + chip) * 2 + which

    mate = dp + 1 - 2 * core
    ahead = lax.rem(dp + 2, n_dp)
    behind = lax.rem(dp + n_dp - 2, n_dp)
    cross = lax.rem(dp + n_dp + 2 * core - 1, n_dp)
    via = at(plane + (z + 2) // RING, lax.rem(z + RING - 3, RING), 1)
    served = lax.rem(z + 3, RING)
    served_from = at(plane - (served + 2) // RING, served, 1)
    drop = at(plane, lax.rem(served + 2, RING), 0)
    brought = at(plane, lax.rem(z + 3, RING), 1)

    sources = (pk_hbm, pv_hbm)

    def part(j):
        return pl.ds(starts[j], sizes[j])

    def own(j, kind):
        return pltpu.make_async_copy(sources[kind].at[part(j)], bufs[j].at[0, kind], own_sem.at[j])

    def own_whole(j):
        return pltpu.make_async_copy(bufs[j].at[1], bufs[j].at[0], own_sem.at[j])

    loads = [
        pltpu.make_async_copy(src, dst, in_sem.at[k])
        for k, (src, dst) in enumerate(
            (
                (parent_hbm, parent_ref),
                (count_hbm, count_ref),
                (q_hbm, q_ref),
                (ck_hbm, ck_ref),
                (cv_hbm, cv_ref),
                (w_hbm, w_ref),
            )
        )
    ]

    barrier = pltpu.get_barrier_semaphore()

    def greet(*others):
        for other in others:
            pl.semaphore_signal(barrier, inc=1, device_id=(other, mp), device_id_type=MESH)

    greet(mate, behind)
    for step in range(1, n_mp):
        pl.semaphore_signal(barrier, inc=1, device_id=(dp, lax.rem(mp + step, n_mp)), device_id_type=MESH)

    def ring_used(owner):
        return lax.rem(owner + 2, RING) == 0 if not DETOUR else owner >= 0

    relayed_to = lax.rem(z + RING - 2, RING)
    sends_via = jnp.logical_and(core == 1, ring_used(z))
    passes_on = jnp.logical_and(core == 1, ring_used(served))
    is_brought = jnp.logical_and(core == 0, ring_used(relayed_to))
    via_late = z < 3
    served_early = z >= RING - 3
    drop_late = z < 3
    brought_early = z >= RING - 3
    no = jnp.logical_not

    def both(*conditions):
        return functools.reduce(jnp.logical_and, conditions)

    pl.when(core == 0)(lambda: greet(cross))
    pl.when(both(sends_via, via_late))(lambda: greet(via))
    pl.when(both(passes_on, no(served_early)))(lambda: greet(served_from))
    pl.when(both(passes_on, drop_late))(lambda: greet(drop))
    pl.when(both(is_brought, no(brought_early)))(lambda: greet(brought))

    for copy in loads:
        copy.start()
    for j in range(chunks):
        for kind in (0, 1):
            own(j, kind).start()
    waits_for = (
        both(sends_via, no(via_late)),
        both(passes_on, served_early),
        both(passes_on, no(drop_late)),
        both(is_brought, brought_early),
    )
    pl.semaphore_wait(barrier, 2 + n_mp - 1 + core + sum(w.astype(jnp.int32) for w in waits_for))

    def tell(other, sem):
        pl.semaphore_signal(sem, inc=1, device_id=(other, mp), device_id_type=MESH)

    pl.when(both(passes_on, served_early))(lambda: tell(served_from, via_ready))
    pl.when(both(is_brought, brought_early))(lambda: tell(brought, drop_ready))

    def remote(src, dst, send, recv, target):
        return pltpu.make_async_remote_copy(
            src_ref=src, dst_ref=dst, send_sem=send, recv_sem=recv, device_id=(target, mp), device_id_type=MESH
        )

    def to_ahead(j, kind):
        return remote(sources[kind].at[part(j)], bufs[j].at[2, kind], z_sem.at[j], recv_sem.at[1, j], ahead)

    def own_to_mate(j, kind):
        return remote(sources[kind].at[part(j)], bufs[j].at[1, kind], d2d_sem.at[j], recv_sem.at[0, j], mate)

    def own_to_via(j, kind):
        return remote(sources[kind].at[part(j)], relays[j].at[kind], out_sem.at[j], relay_sem.at[j], via)

    def two_to_mate(j, slot):
        return remote(bufs[j].at[2], bufs[j].at[slot], fwd_sem.at[j], recv_sem.at[slot - 1, j], mate)

    def two_to_next(j):
        return remote(bufs[j].at[2], bufs[j].at[3], d2d_sem.at[j], recv_sem.at[2, j], cross)

    def relay_on(j):
        return remote(relays[j], bufs[j].at[3], pass_sem.at[j], recv_sem.at[2, j], drop)

    def whole(j, send, recv):
        return remote(bufs[j].at[2], bufs[j].at[1], send, recv, mate)

    def wait_slot(j, slot):
        whole(j, z_sem.at[j], recv_sem.at[slot - 1, j]).wait_recv()

    def wait_sent(j, sem):
        whole(j, sem.at[j], recv_sem.at[0, j]).wait_send()

    def on_ring(j, owner, do):
        if j in DETOUR:
            do()
        else:
            pl.when(lax.rem(owner + 2, RING) == 0)(do)

    def off_ring(j, owner, do):
        if j not in DETOUR:
            pl.when(lax.rem(owner + 2, RING) != 0)(do)

    def start_direct(j):
        for kind in (0, 1):
            to_ahead(j, kind).start()

        @pl.when(core == 0)
        def _():
            for kind in (0, 1):
                own_to_mate(j, kind).start()

    def start_detour(j):
        def do():
            for kind in (0, 1):
                own_to_via(j, kind).start()

        on_ring(j, z, do)

    def pass_on(j):
        def do():
            remote(relays[j], relays[j], out_sem.at[j], relay_sem.at[j], via).wait_recv()
            relay_on(j).start()

        on_ring(j, served, do)

    def forward(j):
        @pl.when(core == 0)
        def _():
            two_to_mate(j, 3).start()

        @pl.when(core == 1)
        def _():
            off_ring(j, lax.rem(z + RING - 1, RING), lambda: two_to_next(j).start())
            two_to_mate(j, 1).start()

    def settle(j):
        wait_sent(j, z_sem)
        wait_sent(j, fwd_sem)

        @pl.when(core == 0)
        def _():
            wait_sent(j, d2d_sem)

        @pl.when(core == 1)
        def _():
            off_ring(j, lax.rem(z + RING - 1, RING), lambda: wait_sent(j, d2d_sem))
            on_ring(j, z, lambda: wait_sent(j, out_sem))
            on_ring(j, served, lambda: wait_sent(j, pass_sem))

    start_direct(0)

    def start_detours():
        for j in range(chunks):
            start_detour(j)

    sends_first = lax.rem(z + 2, RING) == 0
    pl.when(both(sends_via, sends_first))(start_detours)

    for j in range(1, AHEAD):
        start_direct(j)
    most_extra = chunks - AHEAD
    extra = jnp.where(z == RING - 1, most_extra, jnp.maximum(most_extra - EASE * z, 0))
    for j in range(AHEAD, chunks):
        pl.when(extra > j - AHEAD)(functools.partial(start_direct, j))

    for copy in loads:
        copy.wait()

    def cols_of(b):
        return pl.ds(b * COLS, COLS)

    def scaled(c, _):
        for b in range(blocks):
            wide = q_ref[c, cols_of(b)].astype(jnp.float32) * scale
            high = wide.astype(jnp.bfloat16)
            qq_ref[c, cols_of(b), :size] = high
            qq_ref[c, cols_of(b), size:] = (wide - high.astype(jnp.float32)).astype(jnp.bfloat16)
        return 0

    lax.fori_loop(0, slots, scaled, 0)

    def score(c, b, keys, causal):
        n = keys.shape[0]
        s = lax.dot_general(
            jnp.concatenate([keys, keys], axis=1),
            qq_ref[c, cols_of(b)],
            (((1,), (1,)), ((), ())),
            preferred_element_type=jnp.float32,
        )
        if causal:
            key_at = lax.broadcasted_iota(jnp.int32, s.shape, 0)
            row_at = (lax.broadcasted_iota(jnp.int32, s.shape, 1) + b * COLS) // heads
            s = jnp.where(key_at <= row_at, s, NEG)
        s_ref[:n, cols_of(b)] = s
        top_ref[:, cols_of(b)] = jnp.max(s.reshape(n // 8, 8, COLS), axis=0)

    def weigh(c, b, n):
        cols = cols_of(b)
        old = m_ref[c, :, cols]
        peak = jnp.maximum(old, jnp.max(top_ref[:, cols], axis=0, keepdims=True))
        m_ref[c, :, cols] = peak
        alpha_ref[:, cols] = jnp.exp2(old - peak)
        p_ref[:n, cols] = jnp.exp2(s_ref[:n, cols] - peak).astype(jnp.bfloat16)

    def gather(c, b, n):
        cols = cols_of(b)
        acc_ref[c, :, cols] = acc_ref[c, :, cols] * alpha_ref[:, cols] + jnp.dot(
            vt_ref[:, :n], p_ref[:n, cols], preferred_element_type=jnp.float32
        )

    def keep_columns(values):
        vt_ref[:size, : values.shape[0]] = values.T

    def stages(c, n, before, values, scored, keys, causal):
        for b in range(blocks):
            if before:
                gather((c + slots - 1) % slots, b, before)
            weigh(c, b, n)
            if keys is not None:
                score(scored, b, keys, causal)
        keep_columns(values)

    def zero(c, _):
        acc_ref[c] = jnp.zeros(acc_ref.shape[1:], jnp.float32)
        m_ref[c] = jnp.full(m_ref.shape[1:], NEG, jnp.float32)
        return 0

    lax.fori_loop(0, slots, zero, 0)
    vt_ref[size:, :] = jnp.ones((EXTRA, most), jnp.bfloat16)

    group = lax.broadcasted_iota(jnp.int32, member_ref.shape, 0) // heads
    member_ref[...] = (group == lax.broadcasted_iota(jnp.int32, member_ref.shape, 1)).astype(jnp.bfloat16)
    to_row = lax.broadcasted_iota(jnp.int32, (2 * heads, 2 * heads), 0)
    from_row = lax.broadcasted_iota(jnp.int32, (2 * heads, 2 * heads), 1)
    order = (from_row == lax.rem(to_row, heads) * 2 + to_row // heads).astype(jnp.bfloat16)
    w_ref[...] = jnp.dot(order, w_ref[...], preferred_element_type=jnp.float32).astype(jnp.bfloat16)

    head_at = lax.broadcasted_iota(jnp.int32, (heads, rows), 1) % heads
    same = head_at == lax.broadcasted_iota(jnp.int32, (heads, rows), 0)

    def out(c):
        return pltpu.make_async_copy(done_ref.at[c], att_hbm.at[c], done_sem.at[c])

    def finish(c):
        inverse = jnp.where(c < count_ref[0], 1.0 / acc_ref[c, size : size + 1], 0.0)
        done = (acc_ref[c, :size] * inverse).astype(jnp.bfloat16)
        both = jnp.dot(w_ref[...], done, preferred_element_type=jnp.float32)
        for k in (0, 1):
            z_ref[c, k] = jnp.sum(jnp.where(same, both[k * heads : (k + 1) * heads], 0.0), axis=0, keepdims=True)
        done_ref[c] = done.T
        out(c).start()

    for b in range(blocks):
        score(0, b, ck_ref[0], True)

    for c in range(slots - 1):
        stages(c, ck_ref.shape[1], ck_ref.shape[1] if c else 0, cv_ref[c], c + 1, ck_ref[c + 1], True)

    def distance(c):
        return jnp.bitwise_and(dp - parent_ref[0, c], 3)

    def arrive(j):
        own_whole(j).wait()
        wait_slot(j, 1)
        wait_slot(j, 3)

    def cross_over(j):
        end = slots - 1
        values = cv_ref[end] if j == 0 else bufs[j - 1][distance(end), 1]
        keys = None if j == chunks else bufs[j][distance(0), 0]
        stages(end, values.shape[0], values.shape[0], values, 0, keys, False)

    def compute(j):
        arrive(j)
        cross_over(j)
        for c in range(slots - 1):
            earlier = sizes[j] if c else sizes[j - 1] if j else ck_ref.shape[1]
            stages(c, sizes[j], earlier, bufs[j][distance(c), 1], c + 1, bufs[j][distance(c + 1), 0], False)
            if j == chunks - 1 and c >= 1:
                finish(c - 1)

    for j in range(chunks):
        wait_slot(j, 2)
        forward(j)
        for e in range(most_extra - j):
            pl.when(extra == e)(functools.partial(start_direct, j + AHEAD + e))

        if j == 1:
            pl.when(both(sends_via, via_late))(lambda: pl.semaphore_wait(via_ready, 1))
            pl.when(both(sends_via, no(sends_first)))(start_detours)

        if j == 0:

            @pl.when(both(passes_on, drop_late))
            def _():
                pl.semaphore_wait(drop_ready, 1)

        @pl.when(core == 1)
        def _():
            for k in RELAY[j]:
                pass_on(k)

        if j >= 2:
            settle(j - 2)
        if j >= 1:
            compute(j - 1)
    compute(chunks - 1)
    cross_over(chunks)
    finish(slots - 2)
    for b in range(blocks):
        gather(slots - 1, b, sizes[-1])
    finish(slots - 1)

    lanes = z_ref[...].reshape(2 * slots, rows)
    high = lanes.astype(jnp.bfloat16)
    rest = lanes - high.astype(jnp.float32)
    middle = rest.astype(jnp.bfloat16)
    low = (rest - middle.astype(jnp.float32)).astype(jnp.bfloat16)
    sums = jnp.dot(jnp.concatenate([high, middle, low], axis=0), member_ref[...], preferred_element_type=jnp.float32)
    part_ref[...] = sums[: 2 * slots] + sums[2 * slots : 4 * slots] + sums[4 * slots :]

    def to_peer(step):
        return pltpu.make_async_remote_copy(
            src_ref=part_ref,
            dst_ref=gather_ref.at[step - 1],
            send_sem=y_send.at[step - 1],
            recv_sem=y_recv.at[step - 1],
            device_id=(dp, lax.rem(mp + step, n_mp)),
            device_id_type=MESH,
        )

    for step in sorted(range(1, n_mp), key=lambda step: abs(2 * step - n_mp)):
        to_peer(step).start()

    for j in range(max(chunks - 2, 0), chunks):
        settle(j)
    for c in range(slots):
        out(c).wait()
    total = part_ref[...]
    for step in range(1, n_mp):
        to_peer(step).wait_recv()
        total = total + gather_ref[step - 1]
    logit_ref[...] = total
    for step in range(1, n_mp):
        to_peer(step).wait_send()


def place(att_in, logit_in, att_out, logit_out, att_ref, logit_ref, in_sem, out_sem):
    slots = att_in.shape[0]
    pieces = [(logit_in, logit_ref, logit_out)]
    pieces += [(att_in.at[c], att_ref.at[c], att_out.at[c]) for c in range(slots)]
    loads = [pltpu.make_async_copy(src, held, in_sem.at[k]) for k, (src, held, _) in enumerate(pieces)]
    stores = [pltpu.make_async_copy(held, dst, out_sem.at[k]) for k, (_, held, dst) in enumerate(pieces)]
    for load in loads:
        load.start()
    for load, store in zip(loads, stores):
        load.wait()
        store.start()
    for store in stores:
        store.wait()


def solution(mesh):
    n_dp, n_mp = mesh.shape["dp"], mesh.shape["mp"]

    def step(queries, keys, values, prefix_keys, prefix_values, count, parent, weight):
        _, slots, steps, heads, size = queries.shape
        prefix = prefix_keys.shape[1]
        rows = steps * heads
        sizes = [prefix * n // sum(SIZES) for n in SIZES]
        chunks, most = len(sizes), max(sizes)
        bf16, f32 = jnp.bfloat16, jnp.float32
        dma = pltpu.SemaphoreType.DMA
        attended, logits = pl.pallas_call(
            functools.partial(kernel, n_dp, n_mp),
            out_shape=(
                jax.ShapeDtypeStruct((slots, rows, size), bf16),
                jax.ShapeDtypeStruct((2 * slots, steps), f32),
            ),
            in_specs=[pl.BlockSpec(memory_space=pltpu.HBM)] * 8,
            out_specs=(pl.BlockSpec(memory_space=pltpu.HBM), pl.BlockSpec(memory_space=pltpu.VMEM)),
            scratch_shapes=[pltpu.VMEM((4, 2, n, size), bf16) for n in sizes]
            + [pltpu.VMEM((2, n, size), bf16) for n in sizes]
            + [
                pltpu.VMEM((slots, rows, size), bf16),
                pltpu.VMEM((slots, steps, size), bf16),
                pltpu.VMEM((slots, steps, size), bf16),
                pltpu.VMEM((2 * heads, size), bf16),
                pltpu.SMEM((1,), jnp.int32),
                pltpu.SMEM((1, slots), jnp.int32),
                pltpu.VMEM((slots, size + EXTRA, rows), f32),
                pltpu.VMEM((slots, 1, rows), f32),
                pltpu.VMEM((slots, rows, 2 * size), bf16),
                pltpu.VMEM((2 * slots, steps), f32),
                pltpu.VMEM((max(n_mp - 1, 1), 2 * slots, steps), f32),
                pltpu.VMEM((slots, 2, 1, rows), f32),
                pltpu.VMEM((size + EXTRA, most), bf16),
                pltpu.VMEM((rows, steps), bf16),
                pltpu.VMEM((slots, rows, size), bf16),
            ]
            + [
                pltpu.VMEM((most, rows), f32),
                pltpu.VMEM((8, rows), f32),
                pltpu.VMEM((most, rows), bf16),
                pltpu.VMEM((1, rows), f32),
            ]
            + [dma((6,)), dma((chunks,)), dma((3, chunks))]
            + [dma((chunks,))] * 6
            + [dma((slots,))]
            + [dma((max(n_mp - 1, 1),))] * 2
            + [pltpu.SemaphoreType.REGULAR] * 2,
            compiler_params=pltpu.CompilerParams(
                collective_id=0, has_side_effects=True, vmem_limit_bytes=VMEM_LIMIT
            ),
            name="prefix_attention",
        )(
            queries.reshape(slots, rows, size),
            keys.reshape(slots, steps, size),
            values.reshape(slots, steps, size),
            prefix_keys.reshape(prefix, size),
            prefix_values.reshape(prefix, size),
            jnp.transpose(weight, (0, 2, 1)).reshape(2 * heads, size),
            count,
            parent,
        )
        hbm = pl.BlockSpec(memory_space=pltpu.HBM)
        attended, logits = pl.pallas_call(
            place,
            out_shape=(
                jax.ShapeDtypeStruct((slots, rows, size), bf16),
                jax.ShapeDtypeStruct((2 * slots, steps), f32),
            ),
            in_specs=[hbm] * 2,
            out_specs=(hbm, hbm),
            scratch_shapes=[
                pltpu.VMEM((slots, rows, size), bf16),
                pltpu.VMEM((2 * slots, steps), f32),
                dma((slots + 1,)),
                dma((slots + 1,)),
            ],
            compiler_params=pltpu.CompilerParams(vmem_limit_bytes=VMEM_LIMIT),
            name="place",
        )(attended, logits)
        attended = attended.reshape(1, slots, steps, heads, size)
        return attended, jnp.transpose(logits.reshape(slots, 2, steps), (0, 2, 1))[None]

    return jax.shard_map(
        step,
        mesh=mesh,
        in_specs=(
            P("dp", None, None, "mp", None),
            P("dp", None, None, "mp", None),
            P("dp", None, None, "mp", None),
            P("dp", None, "mp", None),
            P("dp", None, "mp", None),
            P("dp"),
            P("dp", None),
            P("mp", None, None),
        ),
        out_specs=(P("dp", None, None, "mp", None), P("dp", None, None, None)),
        check_vma=False,
    )
```
